256 devices in a mesh: node: 8 (over y_hi, x), table: 32 (over y_lo, z, core).
Axes of the slice: x: 4, y: 4 (y_hi: 2, y_lo: 2; y = y_hi * 2 + y_lo), z: 8, core: 2. Of those that a mesh axis runs over, the one named last changes fastest.
Arguments:
- table_rows: float32 [65536, 256], P('table'), may hold values from -6 to 6
- accumulator: float32 [65536], P('table'), may hold values from 1 to 100000
- pooled_replica_rows: int32 [131072, 4, 16], P(('node', 'table')), may hold values from 0 to 4095
- out_grad: bfloat16 [131072, 512], P(('node', 'table')), may hold values from -6 to 6
- weight_in: bfloat16 [1024, 1024], replicated, may hold values from -0.1875 to 0.1875
- weight_out: bfloat16 [1024, 512], replicated, may hold values from -0.1875 to 0.1875
- promote: int32 [32], replicated, may hold values from 0 to 511, as said below
- demote: int32 [8], replicated, may hold values from 0 to 31, as said below
Outputs:
- table_out: float32 [65536, 256], P('table')
- replica_out: float32 [4096, 256], replicated
The draws below stay inside these ranges and needn't reach their ends.
Inputs may be any that keep to these rules, and one draw needn't show every extreme that they name: `promote`: 32 distinct block numbers; block b belongs to table index b // 16. Each table index owns at most 3 of them, and some owns exactly 3. The table indices fall into groups of four consecutive ones that own four of them together. `demote`: distinct slot numbers.
All inputs are finite; a program needn't handle non-finite values.
Results may differ from the reference program's by a relative error of at most 0.0024.
Values sent between devices are 32-bit elements; how exact they have to be, the bound alone decides.
A program may use at most 128 MiB of HBM per device.

```python
import math
import jax
import jax.numpy as jnp
import numpy as np
from jax import lax

E = 256
H = 1024
H2 = 512
F = 4
L = 16
BLOCK = 128
CAP = 3
BLK_DEV = 16
SAMP_DEV = 512
PROMOTED_BLOCKS = 32
HOT_ROWS = 4096
DEMOTED_BLOCKS = 8
ROWS = 65536
SAMPLES = 131072
N_NODE = 8
N_TABLE = 32


def draw_promote(key, part):
    key = jax.random.fold_in(key, 11)
    subkeys = jax.random.split(key, 4)
    groups = PROMOTED_BLOCKS // 4
    patterns = jnp.array([[3, 1, 0, 0], [2, 1, 1, 0], [1, 1, 1, 1], [3, 0, 0, 1]], jnp.int32)
    choose = jax.random.randint(subkeys[0], (groups,), 0, 3).at[0].set(0)
    if groups == 1:
        choose = choose.at[0].set(3)
    else:
        choose = choose.at[groups - 1].set(2)
    scores = jax.random.randint(subkeys[1], (groups, 4), 0, 1 << 20) * 4 + jnp.arange(4, dtype=jnp.int32)[None, :]
    within = jnp.argsort(scores, axis=1)
    within = within.at[0].set(jnp.arange(4, dtype=jnp.int32))
    counts = jnp.take_along_axis(patterns[choose], within, axis=1).reshape(PROMOTED_BLOCKS)
    replica_scores = jax.random.randint(subkeys[2], (PROMOTED_BLOCKS, BLK_DEV), 0, 1 << 20) * BLK_DEV + jnp.arange(BLK_DEV, dtype=jnp.int32)[None, :]
    replica_scores = replica_scores.at[0, 0].set(-1)
    replica_scores = replica_scores.at[PROMOTED_BLOCKS - 1, BLK_DEV - 1].set(-1)
    local_pick = jnp.argsort(replica_scores, axis=1)[:, :CAP]
    global_ids = jnp.arange(PROMOTED_BLOCKS, dtype=jnp.int32)[:, None] * BLK_DEV + local_pick
    present = jnp.arange(CAP, dtype=jnp.int32)[None, :] < counts[:, None]
    slot_scores = jax.random.randint(subkeys[3], (PROMOTED_BLOCKS, CAP), 0, 1 << 20) * (PROMOTED_BLOCKS * CAP) + jnp.arange(PROMOTED_BLOCKS * CAP, dtype=jnp.int32).reshape(PROMOTED_BLOCKS, CAP)
    order_keys = jnp.where(present, slot_scores, slot_scores + (1 << 30))
    selected_blocks = jnp.argsort(order_keys.reshape(-1))[:PROMOTED_BLOCKS]
    return global_ids.reshape(-1)[selected_blocks].astype(jnp.int32)


def draw_demote(key, part):
    key = jax.random.fold_in(key, 12)
    subkeys = jax.random.split(key, 2)
    middle = jax.random.permutation(subkeys[0], PROMOTED_BLOCKS - 2)[:DEMOTED_BLOCKS - 2].astype(jnp.int32) + 1
    ends = jnp.array([0, PROMOTED_BLOCKS - 1], jnp.int32)
    listed = jnp.concatenate([ends, middle])
    order = jax.random.permutation(subkeys[1], DEMOTED_BLOCKS)
    return listed[order].astype(jnp.int32)


def with_ends(drawn, stream_key, low, top_value):
    extent = drawn.shape
    place = [jax.random.randint(jax.random.fold_in(stream_key, axis), (), 0, extent[axis]) for axis in range(len(extent))]
    drawn = drawn.at[tuple(place)].set(low)
    longest = extent.index(max(extent))
    place[longest] = (place[longest] + 1) % extent[longest]
    return drawn.at[tuple(place)].set(top_value)


def level_of(own_key, extent, cuts, low, high):
    def one(dim, blocks):
        heights = jax.random.uniform(jax.random.fold_in(jax.random.fold_in(own_key, 6), dim), (blocks,), jnp.float32, low / len(cuts), high / len(cuts))
        return jnp.repeat(jnp.exp(heights), extent[dim] // blocks).reshape((-1,) + (1,) * (len(extent) - dim - 1))

    gain = one(*cuts[0])
    for cut in cuts[1:]:
        gain = gain * one(*cut)
    return gain


def rank_table(count, skew):
    weights = [(1 << 20) // math.isqrt(grade ** skew) + 1 for grade in range(1, count + 1)]
    scale = 1 + sum(weights) // (1 << 30)
    return np.cumsum(np.array([max(1, weight // scale) for weight in weights]))


def ranked_ids(key, dims, amount, lean):
    grid = rank_table(amount, lean)
    pick = jax.random.randint(jax.random.fold_in(key, 1), dims, 0, int(grid[amount - 1]))
    standing = jnp.searchsorted(jnp.asarray(grid, jnp.int32), pick, side="right")
    return jax.random.permutation(jax.random.fold_in(key, 2), amount)[standing].astype(jnp.int32)


def gaussian(own_key, dims, width, most, cuts=(), kind=jnp.bfloat16):
    values = width * jax.random.normal(own_key, dims, jnp.float32)
    if cuts:
        values = values * level_of(own_key, dims, cuts, -0.22, 0.18)
    return jnp.clip(values, -most, most).astype(kind)


def setup_inputs(seed: int = 0) -> dict:
    splits = jax.random.split(jax.random.key(seed), 9)
    table_rows = gaussian(splits[0], (ROWS, E), 1.0, 6.0, ((0, 32),), jnp.float32)
    accumulator = jnp.clip(jnp.exp(math.log(100000.0) - 11.512925 * jax.random.uniform(splits[1], (ROWS,), jnp.float32) ** level_of(splits[1], (ROWS,), ((0, 32),), -0.2, 0.2)), 1.0, 100000.0)
    pooled_replica_rows = with_ends(ranked_ids(splits[2], (SAMPLES, F, L), HOT_ROWS, 2), jax.random.fold_in(splits[2], 3), 0, HOT_ROWS - 1).astype(jnp.int32)
    out_grad = gaussian(splits[3], (SAMPLES, H2), 1.0, 6.0, ((0, 256),))
    weight_in = gaussian(splits[4], (F * E, H), (F * E) ** -0.5, 0.1875)
    weight_out = gaussian(splits[5], (H, H2), H ** -0.5, 0.1875)
    promote = draw_promote(jax.random.fold_in(splits[8], 71), 0)
    demote = draw_demote(jax.random.fold_in(splits[8], 71), 0)
    return dict(table_rows=table_rows, accumulator=accumulator, pooled_replica_rows=pooled_replica_rows, out_grad=out_grad, weight_in=weight_in, weight_out=weight_out, promote=promote, demote=demote)


learn_rate = 0.5

def local_gradient(hot_low, piece_ids, piece_grad, weight_in, weight_out):
    samples = piece_ids.shape[0]
    row_width = hot_low.shape[1]
    looked = hot_low[piece_ids]
    pooled = lax.optimization_barrier(jnp.sum(looked, axis=2, dtype=jnp.float32)).astype(jnp.bfloat16)
    pooled = pooled.reshape(samples, -1)
    pre_act = jnp.dot(pooled, weight_in, preferred_element_type=jnp.float32)
    back_hidden = jnp.dot(piece_grad, weight_out.T, preferred_element_type=jnp.float32)
    sigmoid_pre = jax.nn.sigmoid(pre_act)
    back_pre = (back_hidden * sigmoid_pre * (1.0 + pre_act * (1.0 - sigmoid_pre))).astype(jnp.bfloat16)
    back_pooled = jnp.dot(back_pre, weight_in.T, preferred_element_type=jnp.float32).astype(jnp.bfloat16)
    back_pooled = back_pooled.reshape(-1, 1, row_width).astype(jnp.float32)
    pooled_count = piece_ids.shape[2]
    spread = jnp.broadcast_to(back_pooled, (back_pooled.shape[0], pooled_count, row_width)).reshape(-1, row_width)
    return jax.ops.segment_sum(spread, piece_ids.reshape(-1), num_segments=hot_low.shape[0])

def adagrad(rows_now, current_state, gradient):
    new_state = current_state + lax.optimization_barrier(jnp.mean(gradient * gradient, axis=1))
    return rows_now - learn_rate * gradient / jnp.sqrt(new_state)[:, None]

def reference(table_rows, accumulator, pooled_replica_rows, out_grad, weight_in, weight_out, promote, demote):
    row_width = table_rows.shape[1]
    table_blocks = table_rows.reshape(-1, BLOCK, row_width)
    hot_rows = table_blocks[promote].reshape(HOT_ROWS, row_width)
    promoted_state = accumulator.reshape(-1, BLOCK)[promote].reshape(HOT_ROWS)
    hot_low = hot_rows.astype(jnp.bfloat16)
    pieces = N_NODE * N_TABLE
    ids_blocked = pooled_replica_rows.reshape(pieces, SAMP_DEV, F, L)
    grads_blocked = out_grad.reshape(pieces, SAMP_DEV, H2)

    def one_piece(running, inputs):
        piece_ids, piece_grad = inputs
        return (running + local_gradient(hot_low, piece_ids, piece_grad, weight_in, weight_out), None)
    gradient, spare_blocks = lax.scan(one_piece, jnp.zeros((HOT_ROWS, row_width), jnp.float32), (ids_blocked, grads_blocked))
    new_hot = adagrad(hot_rows, promoted_state, gradient)
    new_blocks = new_hot.reshape(PROMOTED_BLOCKS, BLOCK, row_width)
    slot_ids = jnp.arange(PROMOTED_BLOCKS, dtype=jnp.int32)
    dropped = jnp.any(demote[None, :] == slot_ids[:, None], axis=1)
    replica_out = jnp.where(dropped[:, None, None], jnp.zeros_like(new_blocks), new_blocks).reshape(HOT_ROWS, row_width)
    table_out = table_blocks.at[promote[demote]].set(new_blocks[demote]).reshape(ROWS, row_width)
    return (table_out, replica_out)
```

```python
import functools

import jax
import jax.numpy as jnp
from jax import lax
from jax.experimental import pallas as pl
from jax.experimental.pallas import tpu as pltpu
from jax.sharding import PartitionSpec as P

MESH = pl.DeviceIdType.MESH
BLOCK = 128
NX, NY, NZ, NC = 4, 4, 8, 2
CHIPS = NX * NY * NZ
TILES = (4, NC, CHIPS, 8, 128)
learn_rate = 0.5
MIB = 1 << 20


def place():
    node = lax.axis_index("node")
    table = lax.axis_index("table")
    yhi, x = node // NX, node % NX
    ylo, rest = table // (NZ * NC), table % (NZ * NC)
    return x, yhi * 2 + ylo, rest // NC, rest % NC


def device(x, y, z, c):
    return ((y // 2) * NX + x, (y % 2) * (NZ * NC) + z * NC + c)


class Torus:
    def __init__(self):
        self.x, self.y, self.z, self.c = place()
        x, y, z, c = self.x, self.y, self.z, self.c
        self.u = jnp.where(c == 0, x, y)
        self.v = jnp.where(c == 0, y, x)
        zs = (NZ, z, self.along_z)
        xs = (NX, x, self.along_x)
        ys = (NY, y, self.along_y)
        us = (NX, self.u, self.along_u)
        vs = (NX, self.v, self.along_v)
        self.parts = ((xs, ys, zs), (ys, xs, zs), (zs, ys, xs), (us, vs, zs))

    def along_x(self, d):
        return device((self.x + d) % NX, self.y, self.z, self.c)

    def along_y(self, d):
        return device(self.x, (self.y + d) % NY, self.z, self.c)

    def along_z(self, d):
        return device(self.x, self.y, (self.z + d) % NZ, self.c)

    def along_u(self, d):
        c = self.c
        return device((self.x + d * (1 - c)) % NX, (self.y + d * c) % NY, self.z, c)

    def along_v(self, d):
        c = self.c
        return device((self.x + d * c) % NX, (self.y + d * (1 - c)) % NY, self.z, c)

    def partner(self):
        return device(self.x, self.y, self.z, 1 - self.c)

    def tile(self, p):
        (na, a, _), (nb, b, _), (nc, c, _) = self.parts[p]
        return (a * nb + b) * nc + c

    def barrier(self, more=()):
        sem = pltpu.get_barrier_semaphore()
        others = [self.along_x(d) for d in range(1, NX)]
        others += [self.along_y(d) for d in range(1, NY)]
        others += [self.along_z(d) for d in range(1, NZ)]
        others += [self.partner()]
        others += list(more)
        for other in others:
            pl.semaphore_signal(sem, inc=1, device_id=other, device_id_type=MESH)
        pl.semaphore_wait(sem, len(others))


class Sender:
    def __init__(self, send, recv):
        self.send, self.recv, self.next, self.all = send, recv, 0, []

    def start(self, src, dst, to):
        k = self.next
        self.next += 1
        copy = pltpu.make_async_remote_copy(
            src_ref=src, dst_ref=dst, send_sem=self.send.at[k], recv_sem=self.recv.at[k],
            device_id=to, device_id_type=MESH,
        )
        copy.start()
        self.all.append(copy)
        return copy

    def drain(self):
        for copy in self.all:
            copy.wait_send()


def ring_blocks(n):
    return n // 2


def gather_all(torus, out, sender):
    c = torus.c
    inner = []
    for p in range(4):
        n, _, along = torus.parts[p][2]
        ref = out.at[p, c, torus.tile(p)]
        inner.append([sender.start(ref, ref, along(d)) for d in range(1, n)])
    middle = []
    for p in range(4):
        for copy in inner[p]:
            copy.wait_recv()
        _, (n, _, along), (size, me, _) = torus.parts[p]
        ref = out.at[p, c, pl.ds(torus.tile(p) - me, size)]
        middle.append([sender.start(ref, ref, along(d)) for d in range(1, n)])
    core = []
    ring = [None] * 4

    def block(p, d, half=None):
        (n, me, _), (nb, _, _), (nc, _, _) = torus.parts[p]
        size = nb * nc
        first = ((me + d + n) % n) * size
        if half is not None:
            size //= 2
            first = first + half * size
        return out.at[p, c, pl.ds(first, size)]

    def forward(p, d):
        ref = block(p, d)
        core.append(sender.start(ref, ref, torus.partner()))

    def step(p, s):
        n, _, along = torus.parts[p][0]
        if ring[p] is not None:
            for copy in ring[p]:
                copy.wait_recv()
        if s < n // 2:
            right, left = block(p, -(s - 1)), block(p, s - 1)
        else:
            right, left = block(p, -(s - 1), 0), block(p, s - 1, 1)
        ring[p] = [sender.start(right, right, along(1)), sender.start(left, left, along(-1))]
        forward(p, -(s - 1))
        if s > 1:
            forward(p, s - 1)

    def last(p):
        for copy in ring[p]:
            copy.wait_recv()
        forward(p, torus.parts[p][0][0] // 2)

    for p in (0, 1, 3, 2):
        for copy in middle[p]:
            copy.wait_recv()
        step(p, 1)
    step(2, 2)
    for p in (0, 1, 3):
        step(p, 2)
    step(2, 3)
    step(2, 4)
    for p in (0, 1, 3, 2):
        last(p)
    for copy in core:
        copy.wait_recv()
    sender.drain()


GATHER_COPIES = 3 * 7 + 3 + 4 * 3 + 3 * 4 + 8 + 3 * 4 + 8


def fetch_kernel(sorted_ref, table_ref, state_ref, out, mine, rows, outgo, income, local_sem, send, recv):
    torus = Torus()
    x, y, z, c = torus.x, torus.y, torus.z, torus.c
    node = (y // 2) * NX + x
    table = (y % 2) * (NZ * NC) + z * NC + c
    first = (table // 4) * 4
    here = table % 4
    blk_count = rows.shape[0]
    pull = pltpu.make_async_copy(table_ref.at[:, node], rows, local_sem)
    pull.start()
    group = [(node, first + (here + d) % 4) for d in range(1, 4)]
    torus.barrier([device(x, y, (z // 2) * 2 + (1 - z % 2), 1 - c)])
    sender = Sender(send, recv)
    pull.wait()
    for j in range(4):
        local = jnp.clip(sorted_ref[first + j] - table * blk_count, 0, blk_count - 1)
        block = rows[local]
        for p in range(4):
            h, w = p // 2, p % 2
            outgo[j, p] = block[h * 8:h * 8 + 8, w * 128:w * 128 + 128]
        outgo[j, 4] = jnp.broadcast_to(state_ref[pl.ds(local, 1), :], (8, 128))
    copies = [
        sender.start(outgo.at[(here + d) % 4], income.at[here], group[d - 1]) for d in range(1, 4)
    ]
    income[here] = outgo[here]
    for copy in copies:
        copy.wait_recv()
    source = (sorted_ref[table] // blk_count) % 4
    got = income[source]
    lane = lax.broadcasted_iota(jnp.int32, (8, 128), 1)
    sub = lax.broadcasted_iota(jnp.int32, (8, 128), 0)
    for p in range(4):
        out[p, c, torus.tile(p)] = got[p]
        mine[p] = got[p]
    for h in range(2):
        own = jnp.where(lane == node * 16 + h * 8 + sub, got[4], 0.0)
        mine[4 + h] = jnp.broadcast_to(jnp.sum(own, axis=1, keepdims=True), (8, 128))
    gather_all(torus, out, sender)


def fetch(sorted_blocks, table_rows, accumulator):
    blk_count = table_rows.shape[0] // BLOCK
    count = GATHER_COPIES + 3
    return pl.pallas_call(
        fetch_kernel,
        out_shape=(
            jax.ShapeDtypeStruct(TILES, jnp.float32),
            jax.ShapeDtypeStruct((6, 8, 128), jnp.float32),
        ),
        in_specs=[
            pl.BlockSpec(memory_space=pltpu.SMEM),
            pl.BlockSpec(memory_space=pl.ANY),
            pl.BlockSpec(memory_space=pltpu.VMEM),
        ],
        out_specs=(pl.BlockSpec(memory_space=pltpu.VMEM), pl.BlockSpec(memory_space=pltpu.VMEM)),
        scratch_shapes=[
            pltpu.VMEM((blk_count, 16, 256), jnp.float32),
            pltpu.VMEM((4, 5, 8, 128), jnp.float32),
            pltpu.VMEM((4, 5, 8, 128), jnp.float32),
            pltpu.SemaphoreType.DMA,
            pltpu.SemaphoreType.DMA((count,)),
            pltpu.SemaphoreType.DMA((count,)),
        ],
        compiler_params=pltpu.CompilerParams(
            collective_id=0, has_side_effects=True, vmem_limit_bytes=40 * MIB
        ),
        name="fetch",
    )(sorted_blocks, table_rows.reshape(blk_count, 8, 16, 256), accumulator.reshape(blk_count, BLOCK))


def tile_of(p, x, y, z, c):
    if p == 2:
        return (z * NY + y) * NX + x
    swap = p == 1 or (p == 3 and c == 1)
    a, b = (y, x) if swap else (x, y)
    return (a * 4 + b) * NZ + z


def compute_kernel(
    ids_ref, order_ref, hot_hbm, grad_hbm, win_hbm, wout_hbm, table_hbm,
    out, table_out,
    hot, dout, win, wout, ids_s, key_s, lo_s, counts, low, pooled, back_t, sems,
):
    f_count, l_count, samples = ids_ref.shape
    copies = [
        pltpu.make_async_copy(src, dst, sems.at[k])
        for k, (src, dst) in enumerate(
            ((hot_hbm, hot), (grad_hbm, dout), (win_hbm, win), (wout_hbm, wout), (table_hbm, table_out))
        )
    ]
    for copy in copies:
        copy.start()

    ids = ids_ref[...].reshape(f_count * l_count, samples)
    slot = ids >> 7
    moved = jnp.zeros_like(slot)
    for s in range(32):
        moved = jnp.where(slot == s, order_ref[s] * BLOCK, moved)
    ids_s[...] = moved + (ids & (BLOCK - 1))

    lane = lax.broadcasted_iota(jnp.int32, (8, 128), 1)
    for f in range(f_count):
        for t in range(samples // 128):
            for half in range(2):
                row = jnp.zeros((8, 128), jnp.int32)
                for k in range(8):
                    l = half * 8 + k
                    one = jnp.broadcast_to(
                        ids_s[f * l_count + l:f * l_count + l + 1, t * 128:t * 128 + 128], (8, 128)
                    )
                    turned = pltpu.roll(one, 0, 1, stride=16, stride_axis=0)
                    turned = pltpu.roll(turned, k * 16, 1)
                    row = jnp.where(lane // 16 == k, turned, row)
                g = f * (samples // 16) + t * 8
                key_s[g:g + 8, half * 128:half * 128 + 128] = (row >> 8) * 16 + lane % 16
                lo_s[g:g + 8, half * 128:half * 128 + 128] = row & 255

    spot = lax.broadcasted_iota(jnp.int32, (256, 256), 0)

    def build(g, carry):
        key = key_s[pl.ds(g, 1), :]
        lo = lo_s[pl.ds(g, 1), :]
        one = jnp.where(spot == key, 1.0, 0.0).astype(jnp.bfloat16)
        two = jnp.where(spot == lo, 1.0, 0.0).astype(jnp.bfloat16)
        table = lax.dot_general(
            one, two, (((1,), (1,)), ((), ())), preferred_element_type=jnp.float32
        ).astype(jnp.bfloat16)
        row = pl.multiple_of((g // 8 * 8 + (8 - g % 8) % 8) * 16, 16)
        for hi in range(16):
            counts[pl.ds(row, 16), hi * 256:hi * 256 + 256] = table[hi * 16:hi * 16 + 16]
        return carry

    lax.fori_loop(0, f_count * samples // 16, build, 0)

    copies[0].wait()
    for q in range(32):
        ylo, z, c = q // 16, q // 2 % 8, q % 2
        for n in range(8):
            x, y = n % 4, (n // 4) * 2 + ylo
            for w in range(2):
                pair = [hot[h * 2 + w, c, tile_of(h * 2 + w, x, y, z, c)] for h in range(2)]
                low[q * 128 + n * 16:q * 128 + n * 16 + 16, w * 128:w * 128 + 128] = jnp.concatenate(
                    pair, axis=0
                ).astype(jnp.bfloat16)

    def pool(m, carry):
        rows = pl.ds(pl.multiple_of(m * 256, 256), 256)
        pooled[rows, :] = jnp.dot(
            counts[rows, :], low[...], preferred_element_type=jnp.float32
        ).astype(jnp.bfloat16)
        return carry

    lax.fori_loop(0, f_count * samples // 256, pool, 0)

    for copy in copies[1:4]:
        copy.wait()
    nt = (((1,), (1,)), ((), ()))

    def dense(m, carry):
        start = pl.multiple_of(m * 256, 256)
        back = lax.dot_general(dout[pl.ds(start, 256), :], wout[...], nt, preferred_element_type=jnp.float32)
        pre = jnp.zeros((256, win.shape[1]), jnp.float32)
        for f in range(f_count):
            part = pooled[pl.ds(pl.multiple_of(f * samples + start, 256), 256), :]
            pre = pre + jnp.dot(part, win[f * 256:f * 256 + 256, :], preferred_element_type=jnp.float32)
        sig = jax.nn.sigmoid(pre)
        back_pre = (back * sig * (1.0 + pre * (1.0 - sig))).astype(jnp.bfloat16)
        for f in range(f_count):
            back_t[f * (samples // 256) + m] = lax.dot_general(
                win[f * 256:f * 256 + 256, :], back_pre, nt, preferred_element_type=jnp.float32
            ).astype(jnp.bfloat16)
        return carry

    lax.fori_loop(0, samples // 256, dense, 0)

    for b in range(16):
        total = jnp.zeros((256, 256), jnp.float32)
        for m in range(f_count * samples // 256):
            total = total + jnp.dot(
                back_t[m], counts[m * 256:m * 256 + 256, b * 256:b * 256 + 256],
                preferred_element_type=jnp.float32,
            )
        rows = total.T
        for k in range(32):
            row = b * 256 + k * 8
            q, n, h = row // 128, row % 128 // 16, k % 2
            ylo, z, c = q // 16, q // 2 % 8, q % 2
            x, y = n % 4, (n // 4) * 2 + ylo
            for w in range(2):
                p = h * 2 + w
                out[p, c, tile_of(p, x, y, z, c)] = rows[k * 8:k * 8 + 8, w * 128:w * 128 + 128]
    copies[4].wait()


def compute(ids, order, hot, out_grad, weight_in, weight_out, table_rows):
    f_count, l_count, samples = ids.shape
    pairs = f_count * samples
    hot_rows = 32 * BLOCK
    return pl.pallas_call(
        compute_kernel,
        out_shape=(
            jax.ShapeDtypeStruct(TILES, jnp.float32),
            jax.ShapeDtypeStruct(table_rows.shape, jnp.float32),
        ),
        in_specs=[
            pl.BlockSpec(memory_space=pltpu.VMEM),
            pl.BlockSpec(memory_space=pltpu.SMEM),
        ] + [pl.BlockSpec(memory_space=pl.ANY)] * 5,
        out_specs=(pl.BlockSpec(memory_space=pltpu.VMEM), pl.BlockSpec(memory_space=pl.ANY)),
        scratch_shapes=[
            pltpu.VMEM(TILES, jnp.float32),
            pltpu.VMEM(out_grad.shape, jnp.bfloat16),
            pltpu.VMEM(weight_in.shape, jnp.bfloat16),
            pltpu.VMEM(weight_out.shape, jnp.bfloat16),
            pltpu.VMEM((f_count * l_count, samples), jnp.int32),
            pltpu.VMEM((pairs // 16, 256), jnp.int32),
            pltpu.VMEM((pairs // 16, 256), jnp.int32),
            pltpu.VMEM((pairs, hot_rows), jnp.bfloat16),
            pltpu.VMEM((hot_rows, 256), jnp.bfloat16),
            pltpu.VMEM((pairs, 256), jnp.bfloat16),
            pltpu.VMEM((pairs // 256, 256, 256), jnp.bfloat16),
            pltpu.SemaphoreType.DMA((5,)),
        ],
        compiler_params=pltpu.CompilerParams(vmem_limit_bytes=56 * MIB),
        name="compute",
    )(ids, order, hot, out_grad, weight_in, weight_out, table_rows)


def scatter_all(torus, grad, acc, core_in, ring_xy, ring_z, mid_in, mid_z, inner_in, inner_z, sender):
    c = torus.c

    def span(p, d, half=None, of_partner=False):
        (n, me, _), (nb, _, _), (nc, _, _) = torus.parts[p]
        if of_partner and p == 3:
            me = torus.v
        size = nb * nc
        first = ((me + d + n) % n) * size
        if half is not None:
            size //= 2
            first = first + half * size
        return pl.ds(first, size)

    def offsets(p):
        n = torus.parts[p][0][0]
        order = [n // 2]
        for d in range(n // 2 - 1, 0, -1):
            order += [d, -d]
        return order + [0]

    core = {}

    def from_core(p, d):
        where = span(p, d, of_partner=True)
        core[p, d] = sender.start(grad.at[p, 1 - c, where], core_in.at[p, where], torus.partner())

    def add_core(p, d):
        core[p, d].wait_recv()
        where = span(p, d)
        acc[p, where] = grad[p, c, where] + core_in[p, where]

    for p in (0, 1, 3, 2):
        from_core(p, offsets(p)[0])
    for p in (2, 0, 1, 3):
        for d in offsets(p)[1:3]:
            from_core(p, d)
    for p in (2, 0, 1, 3):
        for d in offsets(p)[3:]:
            from_core(p, d)

    ring = [None] * 4
    slot = {0: 0, 1: 1, 3: 2}

    def buffers(p, s, side):
        n = torus.parts[p][0][0]
        size = torus.parts[p][1][0] * torus.parts[p][2][0]
        if p == 2:
            first = side * (size // 2) if s == 1 else size + (2 * (s - 2) + side) * size
            return ring_z, pl.ds(first, size // 2 if s == 1 else size)
        first = side * (size // 2) if s == 1 else size + side * size
        return ring_xy.at[slot[p]], pl.ds(first, size // 2 if s == 1 else size)

    def step(p, s):
        n, _, along = torus.parts[p][0]
        d = n // 2 - s + 1
        if s == 1:
            add_core(p, d)
            right, left = span(p, d, 0), span(p, d, 1)
        else:
            add_core(p, d)
            add_core(p, -d)
            absorb(p, s)
            right, left = span(p, d), span(p, -d)
        ref, place_r = buffers(p, s, 0)
        _, place_l = buffers(p, s, 1)
        ring[p] = [
            sender.start(acc.at[p, right], ref.at[place_r], along(1)),
            sender.start(acc.at[p, left], ref.at[place_l], along(-1)),
        ]

    def absorb(p, s):
        n = torus.parts[p][0][0]
        d = n // 2 - s + 1
        for copy in ring[p]:
            copy.wait_recv()
        ref, from_left = buffers(p, s - 1, 0)
        _, from_right = buffers(p, s - 1, 1)
        if s == 2:
            into_left, into_right = span(p, d, 0), span(p, -d, 1)
        else:
            into_left, into_right = span(p, d), span(p, -d)
        if d == 0:
            acc[p, into_left] = acc[p, into_left] + ref[from_left] + ref[from_right]
        else:
            acc[p, into_left] = acc[p, into_left] + ref[from_left]
            acc[p, into_right] = acc[p, into_right] + ref[from_right]

    for p in (0, 1, 3, 2):
        step(p, 1)
    step(2, 2)
    for p in (0, 1, 3):
        step(p, 2)
    step(2, 3)
    step(2, 4)
    middle = [None] * 4
    for p in (0, 1, 3, 2):
        add_core(p, 0)
        absorb(p, torus.parts[p][0][0] // 2 + 1)
        (_, a, _), (nb, b, along), (nc, _, _) = torus.parts[p]
        dst = mid_z if p == 2 else mid_in.at[slot[p]]
        middle[p] = [
            sender.start(
                acc.at[p, pl.ds((a * nb + (b + d) % nb) * nc, nc)], dst.at[d - 1], along(d)
            )
            for d in range(1, nb)
        ]
    inner = [None] * 4
    for p in (0, 1, 3, 2):
        (_, a, _), (nb, b, _), (nc, me, along) = torus.parts[p]
        src = mid_z if p == 2 else mid_in.at[slot[p]]
        for copy in middle[p]:
            copy.wait_recv()
        base = (a * nb + b) * nc
        own = pl.ds(base, nc)
        acc[p, own] = acc[p, own] + src[0] + src[1] + src[2]
        dst = inner_z if p == 2 else inner_in.at[slot[p]]
        inner[p] = [
            sender.start(acc.at[p, base + (me + d) % nc], dst.at[d - 1], along(d)) for d in range(1, nc)
        ]
    result = [None] * 4
    for p in (0, 1, 3, 2):
        nc = torus.parts[p][2][0]
        src = inner_z if p == 2 else inner_in.at[slot[p]]
        for copy in inner[p]:
            copy.wait_recv()
        total = acc[p, torus.tile(p)]
        for d in range(nc - 1):
            total = total + src[d]
        result[p] = total
    return result


SCATTER_COPIES = 3 * 4 + 8 + 3 * 4 + 8 + 4 * 3 + 3 * 7 + 3


def update_kernel(
    grad, mine, out, acc, core_in, ring_xy, ring_z, mid_in, mid_z, inner_in, inner_z, send, recv
):
    torus = Torus()
    torus.barrier()
    sender = Sender(send, recv)
    total = scatter_all(
        torus, grad, acc, core_in, ring_xy, ring_z, mid_in, mid_z, inner_in, inner_z, sender
    )
    for h in range(2):
        left, right = total[2 * h], total[2 * h + 1]
        square = jnp.sum(left * left + right * right, axis=1, keepdims=True)
        state = mine[4 + h] + square / 256.0
        root = jnp.sqrt(state)
        for p, value in ((2 * h, left), (2 * h + 1, right)):
            out[p, torus.c, torus.tile(p)] = mine[p] - learn_rate * value / root
    gather_all(torus, out, sender)


def update(grad, mine):
    count = SCATTER_COPIES + GATHER_COPIES
    tile = (8, 128)
    return pl.pallas_call(
        update_kernel,
        out_shape=jax.ShapeDtypeStruct(TILES, jnp.float32),
        in_specs=[pl.BlockSpec(memory_space=pltpu.VMEM)] * 2,
        out_specs=pl.BlockSpec(memory_space=pltpu.VMEM),
        scratch_shapes=[
            pltpu.VMEM((4, CHIPS) + tile, jnp.float32),
            pltpu.VMEM((4, CHIPS) + tile, jnp.float32),
            pltpu.VMEM((3, 96) + tile, jnp.float32),
            pltpu.VMEM((112,) + tile, jnp.float32),
            pltpu.VMEM((3, 3, NZ) + tile, jnp.float32),
            pltpu.VMEM((3, NX) + tile, jnp.float32),
            pltpu.VMEM((3, 7) + tile, jnp.float32),
            pltpu.VMEM((3,) + tile, jnp.float32),
            pltpu.SemaphoreType.DMA((count,)),
            pltpu.SemaphoreType.DMA((count,)),
        ],
        compiler_params=pltpu.CompilerParams(
            collective_id=1, has_side_effects=True, vmem_limit_bytes=40 * MIB
        ),
        name="update",
    )(grad, mine)


def write_kernel(order_ref, promote_ref, demote_ref, table_ref, tiles, table_in, out, table_out, block, sem):
    s = pl.program_id(0)
    q = order_ref[s]
    ylo, z, c = q // 16, q // 2 % 8, q % 2
    dropped = demote_ref[0] == s
    for k in range(1, demote_ref.shape[0]):
        dropped = jnp.logical_or(dropped, demote_ref[k] == s)
    for n in range(8):
        x, y = n % 4, (n // 4) * 2 + ylo
        for p in range(4):
            h, w = p // 2, p % 2
            if p == 3:
                spot = jnp.where(c == 0, tile_of(3, x, y, z, 0), tile_of(3, x, y, z, 1))
            else:
                spot = tile_of(p, x, y, z, 0)
            value = tiles[p, c, spot]
            rows, columns = slice(n * 16 + h * 8, n * 16 + h * 8 + 8), slice(w * 128, w * 128 + 128)
            out[rows, columns] = jnp.where(dropped, 0.0, value)
            block[rows, columns] = value
    target = promote_ref[s]
    blk_count = table_out.shape[0] // BLOCK

    @pl.when(jnp.logical_and(dropped, target // blk_count == table_ref[0]))
    def _():
        row = pl.multiple_of(target % blk_count * BLOCK, BLOCK)
        copy = pltpu.make_async_copy(block, table_out.at[pl.ds(row, BLOCK), :], sem)
        copy.start()
        copy.wait()


def write(order, promote, demote, my_table, tiles, table):
    scalar = pl.BlockSpec(memory_space=pltpu.SMEM)
    return pl.pallas_call(
        write_kernel,
        grid=(32,),
        out_shape=(
            jax.ShapeDtypeStruct((32 * BLOCK, 256), jnp.float32),
            jax.ShapeDtypeStruct(table.shape, jnp.float32),
        ),
        in_specs=[scalar] * 4 + [
            pl.BlockSpec(memory_space=pltpu.VMEM),
            pl.BlockSpec(memory_space=pl.ANY),
        ],
        out_specs=(pl.BlockSpec((BLOCK, 256), lambda s: (s, 0)), pl.BlockSpec(memory_space=pl.ANY)),
        scratch_shapes=[pltpu.VMEM((BLOCK, 256), jnp.float32), pltpu.SemaphoreType.DMA],
        input_output_aliases={5: 1},
        compiler_params=pltpu.CompilerParams(vmem_limit_bytes=40 * MIB),
        name="write",
    )(order, promote, demote, my_table, tiles, table)


def on_device(
    table_rows, accumulator, pooled_replica_rows, out_grad, weight_in, weight_out, promote, demote
):
    order = jnp.sum((promote[None, :] < promote[:, None]).astype(jnp.int32), axis=1)
    places = jnp.arange(promote.shape[0], dtype=jnp.int32)
    sorted_blocks = jnp.sum(jnp.where(order[None, :] == places[:, None], promote[None, :], 0), axis=1)
    hot, mine = fetch(sorted_blocks, table_rows, accumulator)
    ids = jnp.transpose(pooled_replica_rows, (1, 2, 0))
    grad, table = compute(ids, order, hot, out_grad, weight_in, weight_out, table_rows)
    tiles = update(grad, mine)
    my_table = lax.axis_index("table").astype(jnp.int32).reshape(1)
    replica_out, table_out = write(order, promote, demote, my_table, tiles, table)
    return (table_out, replica_out)


def solution(mesh):
    placed = (
        P("table", None),
        P("table"),
        P(("node", "table"), None, None),
        P(("node", "table"), None),
        P(),
        P(),
        P(),
        P(),
    )
    return jax.shard_map(
        on_device, mesh=mesh, in_specs=placed, out_specs=(P("table", None), P()), check_vma=False
    )
```

```python
import jax
import jax.numpy as jnp
from jax import lax
from jax.experimental import pallas as pl
from jax.experimental.pallas import tpu as pltpu
from jax.sharding import PartitionSpec as P

MESH = pl.DeviceIdType.MESH
BLOCK = 128
NX, NY, NZ, NC = 4, 4, 8, 2
SIDE = 4
RING = NY * NZ
CHIPS = NX * RING
WIDTH = 256
TILES = (2, NC, CHIPS, 8, WIDTH)
learn_rate = 0.5
MIB = 1 << 20
NT = (((1,), (1,)), ((), ()))


def device(x, y, z, c):
    return ((y // 2) * NX + x, (y % 2) * (NZ * NC) + z * NC + c)


class Torus:
    def __init__(self):
        self.node = lax.axis_index("node")
        self.table = lax.axis_index("table")
        yhi, self.x = self.node // NX, self.node % NX
        ylo, rest = self.table // (NZ * NC), self.table % (NZ * NC)
        self.y, self.z, self.c = yhi * 2 + ylo, rest // NC, rest % NC
        self.outer = (self.x, self.y)
        self.middle = (self.y, self.x)

    def along_x(self, d):
        return device((self.x + d + NX) % NX, self.y, self.z, self.c)

    def along_y(self, d):
        return device(self.x, (self.y + d + NY) % NY, self.z, self.c)

    def along_z(self, d):
        return device(self.x, self.y, (self.z + d) % NZ, self.c)

    def along_outer(self, p, d):
        return self.along_y(d) if p else self.along_x(d)

    def along_middle(self, p, d):
        return self.along_x(d) if p else self.along_y(d)

    def partner(self):
        return device(self.x, self.y, self.z, 1 - self.c)

    def column(self, p, d=0):
        return (self.outer[p] * SIDE + (self.middle[p] + d) % SIDE) * NZ

    def block(self, p, d, half=None):
        first = ((self.outer[p] + d + SIDE) % SIDE) * RING
        if half is None:
            return pl.ds(first, RING)
        return pl.ds(first + half * (RING // 2), RING // 2)

    def greet(self, more):
        sem = pltpu.get_barrier_semaphore()
        others = [self.along_x(d) for d in range(1, NX)]
        others += [self.along_y(d) for d in range(1, NY)]
        others += [self.along_z(d) for d in range(1, NZ)]
        others += [self.partner()] + more
        for other in others:
            pl.semaphore_signal(sem, inc=1, device_id=other, device_id_type=MESH)
        return sem, len(others)


class Sender:
    def __init__(self, send, recv):
        self.send, self.recv, self.next, self.all = send, recv, 0, []

    def start(self, src, dst, to):
        k = self.next
        self.next += 1
        copy = pltpu.make_async_remote_copy(
            src_ref=src, dst_ref=dst, send_sem=self.send.at[k], recv_sem=self.recv.at[k],
            device_id=to, device_id_type=MESH,
        )
        copy.start()
        self.all.append(copy)
        return copy

    def drain(self):
        for copy in self.all:
            copy.wait_send()


PARTS = (0, 1)


def gather_all(torus, out, sender):
    c = torus.c
    inner, middle, core, ring = {}, {}, {}, {}

    def forward(p, d):
        ref = out.at[p, c, torus.block(p, d)]
        core[p, d] = sender.start(ref, ref, torus.partner())

    def shift(p, d, half, way):
        ref = out.at[p, c, torus.block(p, d, half)]
        ring[p, d, half, way] = sender.start(ref, ref, torus.along_outer(p, way))

    for p in PARTS:
        ref = out.at[p, c, torus.column(p) + torus.z]
        inner[p] = [sender.start(ref, ref, torus.along_z(d)) for d in range(1, NZ)]
    yield "inner"
    for p in PARTS:
        for copy in inner[p]:
            copy.wait_recv()
        ref = out.at[p, c, pl.ds(torus.column(p), NZ)]
        middle[p] = [sender.start(ref, ref, torus.along_middle(p, d)) for d in range(1, SIDE)]
    yield "middle"
    for p in PARTS:
        for copy in middle[p]:
            copy.wait_recv()
        shift(p, 0, 0, 1)
        shift(p, 0, 1, -1)
        shift(p, 0, 1, 1)
        shift(p, 0, 0, -1)
        forward(p, 0)
    yield "own"
    for p in PARTS:
        ring[p, 0, 0, 1].wait_recv()
        shift(p, -1, 0, 1)
        ring[p, 0, 1, -1].wait_recv()
        shift(p, 1, 1, -1)
    for p in PARTS:
        ring[p, 0, 1, 1].wait_recv()
        forward(p, -1)
        ring[p, 0, 0, -1].wait_recv()
        forward(p, 1)
        core[p, 0].wait_recv()
    yield "near"
    for p in PARTS:
        ring[p, -1, 0, 1].wait_recv()
        ring[p, 1, 1, -1].wait_recv()
        forward(p, 2)
        core[p, -1].wait_recv()
        core[p, 1].wait_recv()
    yield "far"
    for p in PARTS:
        core[p, 2].wait_recv()


GATHER_COPIES = 2 * (7 + 3 + 6 + 4)
SCATTER_COPIES = 2 * (4 + 6 + 3 + 7)


def scatter_all(torus, chunk, grad, total, core_in, ring_in, mid_in, inner_in, sender):
    c = torus.c
    core, ring = {}, {}

    def to_core(p, d):
        chunk(p, 1 - c, d)
        where = torus.block(p, d)
        core[p, d] = sender.start(grad.at[p, 1 - c, where], core_in.at[p, where], torus.partner())

    def add_core(p, d):
        core[p, d].wait_recv()
        where = torus.block(p, d)
        total[p, where] = grad[p, c, where] + core_in[p, where]

    def shift(p, d, half, way, spot):
        ring[p, spot] = sender.start(
            total.at[p, torus.block(p, d, half)], ring_in.at[p, spot], torus.along_outer(p, way)
        )

    def absorb(p, d, half, spot):
        ring[p, spot].wait_recv()
        where = torus.block(p, d, half)
        total[p, where] = total[p, where] + ring_in[p, spot]

    for p in PARTS:
        to_core(p, 2)
    for p in PARTS:
        chunk(p, c, 2)
    for p in PARTS:
        to_core(p, 1)
        to_core(p, -1)
        add_core(p, 2)
        shift(p, 2, 0, 1, 0)
        shift(p, 2, 1, -1, 1)
    for p in PARTS:
        chunk(p, c, 1)
        chunk(p, c, -1)
        add_core(p, 1)
        add_core(p, -1)
        shift(p, 1, 1, 1, 2)
        shift(p, -1, 0, -1, 3)
    for p in PARTS:
        to_core(p, 0)
        absorb(p, 1, 0, 0)
        shift(p, 1, 0, 1, 4)
        absorb(p, -1, 1, 1)
        shift(p, -1, 1, -1, 5)
    for p in PARTS:
        chunk(p, c, 0)
    for p in PARTS:
        add_core(p, 0)
        absorb(p, 0, 1, 2)
        absorb(p, 0, 0, 3)
    middle, inner, result = {}, {}, []
    for p in PARTS:
        absorb(p, 0, 0, 4)
        absorb(p, 0, 1, 5)
        middle[p] = [
            sender.start(
                total.at[p, pl.ds(torus.column(p, d), NZ)], mid_in.at[p, d - 1], torus.along_middle(p, d)
            )
            for d in range(1, SIDE)
        ]
    for p in PARTS:
        for copy in middle[p]:
            copy.wait_recv()
        own = pl.ds(torus.column(p), NZ)
        total[p, own] = total[p, own] + mid_in[p, 0] + mid_in[p, 1] + mid_in[p, 2]
        inner[p] = [
            sender.start(
                total.at[p, torus.column(p) + (torus.z + d) % NZ], inner_in.at[p, d - 1], torus.along_z(d)
            )
            for d in range(1, NZ)
        ]
    for p in PARTS:
        for copy in inner[p]:
            copy.wait_recv()
        value = total[p, torus.column(p) + torus.z]
        for d in range(NZ - 1):
            value = value + inner_in[p, d]
        result.append(value)
    return result


def step_kernel(
    sorted_ref, order_ref, ids_ref, state_ref, table_hbm, grad_hbm, win_hbm, wout_hbm,
    out,
    rows, outgo, income, mine, hot, dout, win, wout, ids_s, key_s, lo_s, counts, low, pooled, back, back_t,
    grad, total, core_in, ring_in, mid_in, inner_in, sems, send, recv,
):
    torus = Torus()
    c, node, table = torus.c, torus.node, torus.table
    f_count, l_count, samples = ids_ref.shape
    pairs = f_count * samples
    sender = Sender(send, recv)
    first, here = (table // 4) * 4, table % 4
    sem, greeted = torus.greet([device(torus.x, torus.y, (torus.z // 2) * 2 + (1 - torus.z % 2), 1 - c)])
    pull = pltpu.make_async_copy(table_hbm.at[:, node], rows, sems.at[0])
    pull.start()
    loads = [
        pltpu.make_async_copy(src, dst, sems.at[k])
        for k, src, dst in ((1, grad_hbm, dout), (2, wout_hbm, wout), (3, win_hbm, win))
    ]
    for copy in loads:
        copy.start()

    blk_count = rows.shape[0]
    pull.wait()
    for j in range(4):
        local = jnp.clip(sorted_ref[first + j] - table * blk_count, 0, blk_count - 1)
        block = rows[local]
        outgo[j, 0] = block[0:8]
        outgo[j, 1] = block[8:16]
        state = jnp.broadcast_to(state_ref[pl.ds(local, 1), :], (8, BLOCK))
        outgo[j, 2, :, 0:BLOCK] = state
        outgo[j, 2, :, BLOCK:WIDTH] = state
    pl.semaphore_wait(sem, greeted)
    copies = [
        sender.start(outgo.at[(here + d) % 4], income.at[here], (node, first + (here + d) % 4))
        for d in range(1, 4)
    ]
    income[here] = outgo[here]

    ids = ids_ref[...].reshape(f_count * l_count, samples)
    slot = ids >> 7
    base = jnp.zeros_like(slot)
    for s in range(32):
        q = order_ref[s]
        base = jnp.where(slot == s, (q // 16) * 4096 + (q % 2) * 1024 + (q // 2 % 8) * 8, base)
    ylo, base = base >> 12, base & 4095
    x = (ids >> 4) & 3
    y = ((ids >> 6) & 1) * 2 + ylo
    lower = ((ids >> 3) & 1) == 1
    place = jnp.where(lower, 2048 + y * 256 + x * 64, x * 256 + y * 64)
    ids_s[...] = base + place + (ids & 7)

    lane = lax.broadcasted_iota(jnp.int32, (8, 128), 1)
    for f in range(f_count):
        for t in range(samples // 128):
            for half in range(2):
                row = jnp.zeros((8, 128), jnp.int32)
                for k in range(8):
                    l = half * 8 + k
                    one = jnp.broadcast_to(
                        ids_s[f * l_count + l:f * l_count + l + 1, t * 128:t * 128 + 128], (8, 128)
                    )
                    turned = pltpu.roll(one, 0, 1, stride=16, stride_axis=0)
                    turned = pltpu.roll(turned, k * 16, 1)
                    row = jnp.where(lane // 16 == k, turned, row)
                g = f * (samples // 16) + t * 8
                key_s[g:g + 8, half * 128:half * 128 + 128] = (row >> 8) * 16 + lane % 16
                lo_s[g:g + 8, half * 128:half * 128 + 128] = row & 255

    for copy in copies:
        copy.wait_recv()
    got = income[(sorted_ref[table] // blk_count) % 4]
    sub = lax.broadcasted_iota(jnp.int32, (8, 128), 0)
    for p in PARTS:
        hot[p, c, torus.column(p) + torus.z] = got[p]
        mine[p] = got[p]
        own = jnp.where(lane == node * 16 + p * 8 + sub, got[2, :, 0:BLOCK], 0.0)
        mine[2, :, p * BLOCK:p * BLOCK + BLOCK] = jnp.broadcast_to(
            jnp.sum(own, axis=1, keepdims=True), (8, BLOCK)
        )
    fetch = gather_all(torus, hot, sender)
    spot = lax.broadcasted_iota(jnp.int32, (256, 256), 0)

    def build(g, carry):
        key = key_s[pl.ds(g, 1), :]
        lo = lo_s[pl.ds(g, 1), :]
        one = jnp.where(spot == key, 1.0, 0.0).astype(jnp.bfloat16)
        two = jnp.where(spot == lo, 1.0, 0.0).astype(jnp.bfloat16)
        product = lax.dot_general(one, two, NT, preferred_element_type=jnp.float32).astype(jnp.bfloat16)
        row = pl.multiple_of((g // 8 * 8 + (8 - g % 8) % 8) * 16, 16)
        for hi in range(16):
            counts[pl.ds(row, 16), hi * 256:hi * 256 + 256] = product[hi * 16:hi * 16 + 16]
        return carry

    def pool(p, core, d, start=False):
        block = (torus.outer[p] + d + SIDE) % SIDE
        column = pl.multiple_of(((p * NC + core) * SIDE + block) * 256, 256)
        low[pl.ds(column, 256), :] = hot[p, core, torus.block(p, d)].reshape(256, WIDTH).astype(jnp.bfloat16)

        def one(m, carry):
            spots = pl.ds(pl.multiple_of(m * 256, 256), 256)
            value = jnp.dot(
                counts[spots, pl.ds(column, 256)], low[pl.ds(column, 256), :],
                preferred_element_type=jnp.float32,
            )
            pooled[spots, :] = value if start else pooled[spots, :] + value
            return carry

        lax.fori_loop(0, pairs // 256, one, 0, unroll=2)

    groups = pairs // 16
    next(fetch)
    lax.fori_loop(0, groups // 2, build, 0, unroll=4)
    next(fetch)
    lax.fori_loop(groups // 2, groups, build, 0, unroll=4)
    next(fetch)
    for p in PARTS:
        pool(p, c, 0, start=p == 0)
    loads[0].wait()
    loads[1].wait()

    def project(m, carry):
        spots = pl.ds(pl.multiple_of(m * 256, 256), 256)
        back[spots, :] = lax.dot_general(dout[spots, :], wout[...], NT, preferred_element_type=jnp.float32)
        return carry

    lax.fori_loop(0, samples // 256, project, 0)
    next(fetch)
    for p in PARTS:
        pool(p, c, -1)
        pool(p, c, 1)
        pool(p, 1 - c, 0)
    next(fetch)
    for p in PARTS:
        pool(p, c, 2)
        pool(p, 1 - c, -1)
        pool(p, 1 - c, 1)
    next(fetch, None)
    for p in PARTS:
        pool(p, 1 - c, 2)
    loads[2].wait()

    def dense(m, carry):
        start = pl.multiple_of(m * 256, 256)
        pre = jnp.zeros((256, win.shape[1]), jnp.float32)
        for f in range(f_count):
            part = pooled[pl.ds(pl.multiple_of(f * samples + start, 256), 256), :].astype(jnp.bfloat16)
            pre = pre + jnp.dot(part, win[f * 256:f * 256 + 256, :], preferred_element_type=jnp.float32)
        sig = jax.nn.sigmoid(pre)
        back_pre = (back[pl.ds(start, 256), :] * sig * (1.0 + pre * (1.0 - sig))).astype(jnp.bfloat16)
        for f in range(f_count):
            back_t[f * (samples // 256) + m] = lax.dot_general(
                win[f * 256:f * 256 + 256, :], back_pre, NT, preferred_element_type=jnp.float32
            ).astype(jnp.bfloat16)
        return carry

    lax.fori_loop(0, samples // 256, dense, 0)

    def chunk(p, core, d):
        block = (torus.outer[p] + d + SIDE) % SIDE
        column = pl.multiple_of(((p * NC + core) * SIDE + block) * 256, 256)
        value = jnp.zeros((256, 256), jnp.float32)
        for m in range(pairs // 256):
            value = value + jnp.dot(
                back_t[m], counts[m * 256:m * 256 + 256, pl.ds(column, 256)],
                preferred_element_type=jnp.float32,
            )
        grad[p, core, torus.block(p, d)] = value.T.reshape(RING, 8, WIDTH)

    result = scatter_all(torus, chunk, grad, total, core_in, ring_in, mid_in, inner_in, sender)
    for p in PARTS:
        square = jnp.sum(result[p] * result[p], axis=1, keepdims=True)
        root = jnp.sqrt(mine[2, :, p * BLOCK:p * BLOCK + BLOCK] + square / WIDTH)
        root = jnp.concatenate([root, root], axis=1)
        out[p, c, torus.column(p) + torus.z] = mine[p] - learn_rate * result[p] / root
    for _ in gather_all(torus, out, sender):
        pass
    sender.drain()


def step(sorted_blocks, order, ids, state, table, out_grad, weight_in, weight_out):
    f_count, l_count, samples = ids.shape
    pairs = f_count * samples
    hot_rows = 32 * BLOCK
    count = SCATTER_COPIES + 2 * GATHER_COPIES + 3
    tile = (8, WIDTH)
    f32, bf16, i32 = jnp.float32, jnp.bfloat16, jnp.int32
    scalar, vmem, hbm = (pl.BlockSpec(memory_space=m) for m in (pltpu.SMEM, pltpu.VMEM, pl.ANY))
    return pl.pallas_call(
        step_kernel,
        out_shape=jax.ShapeDtypeStruct(TILES, f32),
        in_specs=[scalar, scalar, vmem, vmem, hbm, hbm, hbm, hbm],
        out_specs=vmem,
        scratch_shapes=[
            pltpu.VMEM((table.shape[0], 16, WIDTH), f32),
            pltpu.VMEM((4, 3) + tile, f32),
            pltpu.VMEM((4, 3) + tile, f32),
            pltpu.VMEM((3,) + tile, f32),
            pltpu.VMEM(TILES, f32),
            pltpu.VMEM(out_grad.shape, bf16),
            pltpu.VMEM(weight_in.shape, bf16),
            pltpu.VMEM(weight_out.shape, bf16),
            pltpu.VMEM((f_count * l_count, samples), i32),
            pltpu.VMEM((pairs // 16, 256), i32),
            pltpu.VMEM((pairs // 16, 256), i32),
            pltpu.VMEM((pairs, hot_rows), bf16),
            pltpu.VMEM((hot_rows, WIDTH), bf16),
            pltpu.VMEM((pairs, WIDTH), f32),
            pltpu.VMEM((samples, weight_in.shape[1]), f32),
            pltpu.VMEM((pairs // 256, 256, 256), bf16),
            pltpu.VMEM(TILES, f32),
            pltpu.VMEM((2, CHIPS) + tile, f32),
            pltpu.VMEM((2, CHIPS) + tile, f32),
            pltpu.VMEM((2, 6, RING // 2) + tile, f32),
            pltpu.VMEM((2, 3, NZ) + tile, f32),
            pltpu.VMEM((2, 7) + tile, f32),
            pltpu.SemaphoreType.DMA((4,)),
            pltpu.SemaphoreType.DMA((count,)),
            pltpu.SemaphoreType.DMA((count,)),
        ],
        compiler_params=pltpu.CompilerParams(
            collective_id=0, has_side_effects=True, vmem_limit_bytes=58 * MIB
        ),
        name="step",
    )(sorted_blocks, order, ids, state, table, out_grad, weight_in, weight_out)


PER_STEP = 4


def write_kernel(order_ref, promote_ref, demote_ref, tiles, table_ref, out, table_out):
    i = pl.program_id(0)

    def rows_of(q, n, h):
        ylo, z, c = q // 16, q // 2 % 8, q % 2
        x, y = n % 4, (n // 4) * 2 + ylo
        a, b = (y, x) if h else (x, y)
        return tiles[h, c, (a * SIDE + b) * NZ + z]

    for k in range(PER_STEP):
        s = i * PER_STEP + k
        q = order_ref[s]
        dropped = demote_ref[0] == s
        for j in range(1, demote_ref.shape[0]):
            dropped = jnp.logical_or(dropped, demote_ref[j] == s)
        for n in range(8):
            for h in range(2):
                first = k * BLOCK + n * 16 + h * 8
                out[first:first + 8, :] = jnp.where(dropped, 0.0, rows_of(q, n, h))

    table_out[...] = table_ref[...]
    count = table_out.shape[0] // BLOCK
    first_block = (lax.axis_index("table") * pl.num_programs(0) + i) * count
    for j in range(demote_ref.shape[0]):
        s = demote_ref[j]
        local = promote_ref[s] - first_block

        @pl.when(jnp.logical_and(local >= 0, local < count))
        def _():
            q = order_ref[s]
            for n in range(8):
                for h in range(2):
                    first = pl.multiple_of(local * BLOCK + n * 16 + h * 8, 8)
                    table_out[pl.ds(first, 8), :] = rows_of(q, n, h)


def write(order, promote, demote, tiles, table):
    steps = 32 // PER_STEP
    scalar = pl.BlockSpec(memory_space=pltpu.SMEM)
    table_block = pl.BlockSpec((table.shape[0] // steps, WIDTH), lambda i: (i, 0))
    return pl.pallas_call(
        write_kernel,
        grid=(steps,),
        out_shape=(
            jax.ShapeDtypeStruct((32 * BLOCK, WIDTH), jnp.float32),
            jax.ShapeDtypeStruct(table.shape, jnp.float32),
        ),
        in_specs=[scalar] * 3 + [pl.BlockSpec(memory_space=pltpu.VMEM), table_block],
        out_specs=(pl.BlockSpec((PER_STEP * BLOCK, WIDTH), lambda i: (i, 0)), table_block),
        compiler_params=pltpu.CompilerParams(vmem_limit_bytes=24 * MIB),
        name="write",
    )(order, promote, demote, tiles, table)


def on_device(
    table_rows, accumulator, pooled_replica_rows, out_grad, weight_in, weight_out, promote, demote
):
    order = jnp.sum((promote[None, :] < promote[:, None]).astype(jnp.int32), axis=1)
    places = jnp.arange(promote.shape[0], dtype=jnp.int32)
    sorted_blocks = jnp.sum(jnp.where(order[None, :] == places[:, None], promote[None, :], 0), axis=1)
    blk_count = table_rows.shape[0] // BLOCK
    ids = jnp.transpose(pooled_replica_rows, (1, 2, 0))
    tiles = step(
        sorted_blocks, order, ids, accumulator.reshape(blk_count, BLOCK),
        table_rows.reshape(blk_count, 8, 16, WIDTH), out_grad, weight_in, weight_out,
    )
    replica_out, table_out = write(order, promote, demote, tiles, table_rows)
    return (table_out, replica_out)


def solution(mesh):
    placed = (
        P("table", None),
        P("table"),
        P(("node", "table"), None, None),
        P(("node", "table"), None),
        P(),
        P(),
        P(),
        P(),
    )
    return jax.shard_map(
        on_device, mesh=mesh, in_specs=placed, out_specs=(P("table", None), P()), check_vma=False
    )
```

```python
import jax
import jax.numpy as jnp
from jax import lax
from jax.experimental import pallas as pl
from jax.experimental.pallas import tpu as pltpu
from jax.sharding import PartitionSpec as P

MESH = pl.DeviceIdType.MESH
BLOCK = 128
NX, NY, NZ, NC = 4, 4, 8, 2
SIDE = 4
RING = NY * NZ
CHIPS = NX * RING
WIDTH = 256
TILES = (2, NC, CHIPS, 8, WIDTH)
learn_rate = 0.5
MIB = 1 << 20
NT = (((1,), (1,)), ((), ()))


def device(x, y, z, c):
    return ((y // 2) * NX + x, (y % 2) * (NZ * NC) + z * NC + c)


class Torus:
    def __init__(self):
        self.node = lax.axis_index("node")
        self.table = lax.axis_index("table")
        yhi, self.x = self.node // NX, self.node % NX
        ylo, rest = self.table // (NZ * NC), self.table % (NZ * NC)
        self.y, self.z, self.c = yhi * 2 + ylo, rest // NC, rest % NC
        self.outer = (self.x, self.y)
        self.middle = (self.y, self.x)

    def along_x(self, d):
        return device((self.x + d + NX) % NX, self.y, self.z, self.c)

    def along_y(self, d):
        return device(self.x, (self.y + d + NY) % NY, self.z, self.c)

    def along_z(self, d):
        return device(self.x, self.y, (self.z + d) % NZ, self.c)

    def along_outer(self, p, d):
        return self.along_y(d) if p else self.along_x(d)

    def along_middle(self, p, d):
        return self.along_x(d) if p else self.along_y(d)

    def partner(self):
        return device(self.x, self.y, self.z, 1 - self.c)

    def column(self, p, d=0):
        return (self.outer[p] * SIDE + (self.middle[p] + d) % SIDE) * NZ

    def block(self, p, d, half=None):
        first = ((self.outer[p] + d + SIDE) % SIDE) * RING
        if half is None:
            return pl.ds(first, RING)
        return pl.ds(first + half * (RING // 2), RING // 2)

    def greet(self, more):
        sem = pltpu.get_barrier_semaphore()
        others = [self.along_x(d) for d in range(1, NX)]
        others += [self.along_y(d) for d in range(1, NY)]
        others += [self.along_z(d) for d in range(1, NZ)]
        others += [self.partner()] + more
        for other in others:
            pl.semaphore_signal(sem, inc=1, device_id=other, device_id_type=MESH)
        return sem, len(others)


class Sender:
    def __init__(self, send, recv):
        self.send, self.recv, self.next, self.all = send, recv, 0, []

    def start(self, src, dst, to):
        k = self.next
        self.next += 1
        copy = pltpu.make_async_remote_copy(
            src_ref=src, dst_ref=dst, send_sem=self.send.at[k], recv_sem=self.recv.at[k],
            device_id=to, device_id_type=MESH,
        )
        copy.start()
        self.all.append(copy)
        return copy

    def drain(self):
        for copy in self.all:
            copy.wait_send()


PARTS = (0, 1)


def gather_all(torus, out, sender):
    c = torus.c
    inner, middle, core, ring = {}, {}, {}, {}

    def forward(p, d):
        ref = out.at[p, c, torus.block(p, d)]
        core[p, d] = sender.start(ref, ref, torus.partner())

    def shift(p, d, half, way):
        ref = out.at[p, c, torus.block(p, d, half)]
        ring[p, d, half, way] = sender.start(ref, ref, torus.along_outer(p, way))

    for p in PARTS:
        ref = out.at[p, c, torus.column(p) + torus.z]
        inner[p] = [sender.start(ref, ref, torus.along_z(d)) for d in range(1, NZ)]
    yield "inner"
    for p in PARTS:
        for copy in inner[p]:
            copy.wait_recv()
        ref = out.at[p, c, pl.ds(torus.column(p), NZ)]
        middle[p] = [sender.start(ref, ref, torus.along_middle(p, d)) for d in range(1, SIDE)]
    yield "middle"
    for p in PARTS:
        for copy in middle[p]:
            copy.wait_recv()
        shift(p, 0, 0, 1)
        shift(p, 0, 1, -1)
        shift(p, 0, 1, 1)
        shift(p, 0, 0, -1)
        forward(p, 0)
    yield "own"
    for p in PARTS:
        ring[p, 0, 0, 1].wait_recv()
        shift(p, -1, 0, 1)
        ring[p, 0, 1, -1].wait_recv()
        shift(p, 1, 1, -1)
    for p in PARTS:
        ring[p, 0, 1, 1].wait_recv()
        forward(p, -1)
        ring[p, 0, 0, -1].wait_recv()
        forward(p, 1)
        core[p, 0].wait_recv()
    yield "near"
    for p in PARTS:
        ring[p, -1, 0, 1].wait_recv()
        ring[p, 1, 1, -1].wait_recv()
        forward(p, 2)
        core[p, -1].wait_recv()
        core[p, 1].wait_recv()
    yield "far"
    for p in PARTS:
        core[p, 2].wait_recv()


GATHER_COPIES = 2 * (7 + 3 + 6 + 4)
SCATTER_COPIES = 2 * (4 + 6 + 3 + 7)


def scatter_all(torus, chunk, grad, total, core_in, ring_in, mid_in, inner_in, sender):
    c = torus.c
    core, ring = {}, {}

    def to_core(p, d):
        chunk(p, 1 - c, d)
        where = torus.block(p, d)
        core[p, d] = sender.start(grad.at[p, 1 - c, where], core_in.at[p, where], torus.partner())

    def add_core(p, d):
        core[p, d].wait_recv()
        where = torus.block(p, d)
        total[p, where] = grad[p, c, where] + core_in[p, where]

    def shift(p, d, half, way, spot):
        ring[p, spot] = sender.start(
            total.at[p, torus.block(p, d, half)], ring_in.at[p, spot], torus.along_outer(p, way)
        )

    def absorb(p, d, half, spot):
        ring[p, spot].wait_recv()
        where = torus.block(p, d, half)
        total[p, where] = total[p, where] + ring_in[p, spot]

    for p in PARTS:
        to_core(p, 2)
    for p in PARTS:
        chunk(p, c, 2)
    for d in (1, -1):
        to_core(0, d)
    to_core(1, 1)
    for p in PARTS:
        add_core(p, 2)
        shift(p, 2, 0, 1, 0)
        shift(p, 2, 1, -1, 1)
    to_core(1, -1)
    for p in PARTS:
        chunk(p, c, 1)
        chunk(p, c, -1)
        add_core(p, 1)
        shift(p, 1, 1, 1, 2)
        add_core(p, -1)
        shift(p, -1, 0, -1, 3)
    for p in PARTS:
        to_core(p, 0)
    for p in PARTS:
        chunk(p, c, 0)
    for p in PARTS:
        absorb(p, 1, 0, 0)
        shift(p, 1, 0, 1, 4)
        absorb(p, -1, 1, 1)
        shift(p, -1, 1, -1, 5)
    for p in PARTS:
        add_core(p, 0)
        absorb(p, 0, 1, 2)
        absorb(p, 0, 0, 3)
    middle, inner, result = {}, {}, []
    for p in PARTS:
        absorb(p, 0, 0, 4)
        absorb(p, 0, 1, 5)
        middle[p] = [
            sender.start(
                total.at[p, pl.ds(torus.column(p, d), NZ)], mid_in.at[p, d - 1], torus.along_middle(p, d)
            )
            for d in range(1, SIDE)
        ]
    for p in PARTS:
        for copy in middle[p]:
            copy.wait_recv()
        own = pl.ds(torus.column(p), NZ)
        total[p, own] = total[p, own] + mid_in[p, 0] + mid_in[p, 1] + mid_in[p, 2]
        inner[p] = [
            sender.start(
                total.at[p, torus.column(p) + (torus.z + d) % NZ], inner_in.at[p, d - 1], torus.along_z(d)
            )
            for d in range(1, NZ)
        ]
    for p in PARTS:
        for copy in inner[p]:
            copy.wait_recv()
        value = total[p, torus.column(p) + torus.z]
        for d in range(NZ - 1):
            value = value + inner_in[p, d]
        result.append(value)
    return result


def step_kernel(
    promote_ref, ids_hbm, state_hbm, table_hbm, grad_hbm, win_hbm, wout_hbm,
    out, order_ref,
    ids_in, state_in, rows, outgo, income, mine, hot, dout, win, wout, ids_s, key_s, lo_s, counts, low, pooled, back, back_t,
    grad, total, core_in, ring_in, mid_in, inner_in, sems, send, recv,
):
    torus = Torus()
    c, node, table = torus.c, torus.node, torus.table
    f_count, l_count, samples = ids_in.shape
    pairs = f_count * samples
    slots = order_ref.shape[0]
    sender = Sender(send, recv)
    first, here = (table // 4) * 4, table % 4
    sem, greeted = torus.greet([device(torus.x, torus.y, (torus.z // 2) * 2 + (1 - torus.z % 2), 1 - c)])
    pull = pltpu.make_async_copy(table_hbm.at[:, node], rows, sems.at[0])
    pull.start()
    small = [
        pltpu.make_async_copy(src, dst, sems.at[k])
        for k, src, dst in ((4, state_hbm, state_in), (5, ids_hbm, ids_in))
    ]
    loads = [
        pltpu.make_async_copy(src, dst, sems.at[k])
        for k, src, dst in ((1, grad_hbm, dout), (2, wout_hbm, wout), (3, win_hbm, win))
    ]
    for copy in small + loads:
        copy.start()

    blk_count = rows.shape[0]
    group = [jnp.int32(1 << 30)] * 4
    for s in range(slots):
        value = promote_ref[s]
        value = jnp.where(value // (4 * blk_count) == table // 4, value, 1 << 30)
        for j in range(4):
            group[j], value = jnp.minimum(group[j], value), jnp.maximum(group[j], value)
    pull.wait()
    small[0].wait()
    for j in range(4):
        local = jnp.clip(group[j] - table * blk_count, 0, blk_count - 1)
        block = rows[local]
        outgo[j, 0] = block[0:8]
        outgo[j, 1] = block[8:16]
        state = jnp.broadcast_to(state_in[pl.ds(local, 1), :], (8, BLOCK))
        outgo[j, 2, :, 0:BLOCK] = state
        outgo[j, 2, :, BLOCK:WIDTH] = state
    pl.semaphore_wait(sem, greeted)
    copies = [
        sender.start(outgo.at[(here + d) % 4], income.at[here], (node, first + (here + d) % 4))
        for d in range(1, 4)
    ]
    income[here] = outgo[here]

    small[1].wait()
    ids = ids_in[...].reshape(f_count * l_count, samples)
    slot = ids >> 7
    block = jnp.zeros_like(slot)
    for s in range(slots):
        block = jnp.where(slot == s, promote_ref[s], block)
    q = jnp.zeros_like(slot)
    for s in range(slots):
        q = q + jnp.where(promote_ref[s] < block, 1, 0)
    ylo, base = q >> 4, (q & 1) * 1024 + ((q >> 1) & 7) * 8
    x = (ids >> 4) & 3
    y = ((ids >> 6) & 1) * 2 + ylo
    lower = ((ids >> 3) & 1) == 1
    place = jnp.where(lower, 2048 + y * 256 + x * 64, x * 256 + y * 64)
    ids_s[...] = base + place + (ids & 7)

    lane = lax.broadcasted_iota(jnp.int32, (8, 128), 1)
    for f in range(f_count):
        for t in range(samples // 128):
            for half in range(2):
                row = jnp.zeros((8, 128), jnp.int32)
                for k in range(8):
                    l = half * 8 + k
                    one = jnp.broadcast_to(
                        ids_s[f * l_count + l:f * l_count + l + 1, t * 128:t * 128 + 128], (8, 128)
                    )
                    turned = pltpu.roll(one, 0, 1, stride=16, stride_axis=0)
                    turned = pltpu.roll(turned, k * 16, 1)
                    row = jnp.where(lane // 16 == k, turned, row)
                g = f * (samples // 16) + t * 8
                key_s[g:g + 8, half * 128:half * 128 + 128] = (row >> 8) * 16 + lane % 16
                lo_s[g:g + 8, half * 128:half * 128 + 128] = row & 255

    for copy in copies:
        copy.wait_recv()
    kept = jnp.where(here == 0, group[0], jnp.where(here == 1, group[1], jnp.where(here == 2, group[2], group[3])))
    got = income[(kept // blk_count) % 4]
    sub = lax.broadcasted_iota(jnp.int32, (8, 128), 0)
    for p in PARTS:
        hot[p, c, torus.column(p) + torus.z] = got[p]
        mine[p] = got[p]
        own = jnp.where(lane == node * 16 + p * 8 + sub, got[2, :, 0:BLOCK], 0.0)
        mine[2, :, p * BLOCK:p * BLOCK + BLOCK] = jnp.broadcast_to(
            jnp.sum(own, axis=1, keepdims=True), (8, BLOCK)
        )
    fetch = gather_all(torus, hot, sender)
    spot = lax.broadcasted_iota(jnp.int32, (256, 256), 0)

    def build(g, carry):
        key = key_s[pl.ds(g, 1), :]
        lo = lo_s[pl.ds(g, 1), :]
        one = jnp.where(spot == key, 1.0, 0.0).astype(jnp.bfloat16)
        two = jnp.where(spot == lo, 1.0, 0.0).astype(jnp.bfloat16)
        product = lax.dot_general(one, two, NT, preferred_element_type=jnp.float32).astype(jnp.bfloat16)
        row = pl.multiple_of((g // 8 * 8 + (8 - g % 8) % 8) * 16, 16)
        for hi in range(16):
            counts[pl.ds(row, 16), hi * 256:hi * 256 + 256] = product[hi * 16:hi * 16 + 16]
        return carry

    def pool(blocks, start=False):
        columns = []
        for p, core, d in blocks:
            block = (torus.outer[p] + d + SIDE) % SIDE
            column = pl.ds(pl.multiple_of(((p * NC + core) * SIDE + block) * 256, 256), 256)
            low[column, :] = hot[p, core, torus.block(p, d)].reshape(256, WIDTH).astype(jnp.bfloat16)
            columns.append(column)

        def one(m, carry):
            spots = pl.ds(pl.multiple_of(m * 256, 256), 256)
            value = None if start else pooled[spots, :]
            for column in columns:
                term = jnp.dot(counts[spots, column], low[column, :], preferred_element_type=jnp.float32)
                value = term if value is None else value + term
            pooled[spots, :] = value
            return carry

        lax.fori_loop(0, pairs // 256, one, 0, unroll=2)

    groups = pairs // 16
    next(fetch)
    early, late = groups * 7 // 16, groups * 7 // 8
    lax.fori_loop(0, early, build, 0, unroll=4)
    next(fetch)
    lax.fori_loop(early, late, build, 0, unroll=4)
    next(fetch)
    lax.fori_loop(late, groups, build, 0, unroll=4)
    pool([(p, c, 0) for p in PARTS], start=True)
    loads[0].wait()
    loads[1].wait()

    def project(m, carry):
        spots = pl.ds(pl.multiple_of(m * 256, 256), 256)
        back[spots, :] = lax.dot_general(dout[spots, :], wout[...], NT, preferred_element_type=jnp.float32)
        return carry

    lax.fori_loop(0, samples // 256, project, 0)

    def rank(s, carry):
        total = jnp.int32(0)
        for other in range(slots):
            total = total + jnp.where(promote_ref[other] < promote_ref[s], 1, 0)
        order_ref[s] = total
        return carry

    lax.fori_loop(0, slots, rank, 0)
    next(fetch)
    pool([(p, core, d) for p in PARTS for core, d in ((c, -1), (c, 1), (1 - c, 0))])
    next(fetch)
    pool([(p, core, d) for p in PARTS for core, d in ((c, 2), (1 - c, -1), (1 - c, 1))])
    next(fetch, None)
    pool([(p, 1 - c, 2) for p in PARTS])
    loads[2].wait()

    def dense(m, carry):
        start = pl.multiple_of(m * 256, 256)
        pre = jnp.zeros((256, win.shape[1]), jnp.float32)
        for f in range(f_count):
            part = pooled[pl.ds(pl.multiple_of(f * samples + start, 256), 256), :].astype(jnp.bfloat16)
            pre = pre + jnp.dot(part, win[f * 256:f * 256 + 256, :], preferred_element_type=jnp.float32)
        sig = jax.nn.sigmoid(pre)
        back_pre = (back[pl.ds(start, 256), :] * sig * (1.0 + pre * (1.0 - sig))).astype(jnp.bfloat16)
        for f in range(f_count):
            back_t[f * (samples // 256) + m] = lax.dot_general(
                win[f * 256:f * 256 + 256, :], back_pre, NT, preferred_element_type=jnp.float32
            ).astype(jnp.bfloat16)
        return carry

    lax.fori_loop(0, samples // 256, dense, 0)

    def chunk(p, core, d):
        block = (torus.outer[p] + d + SIDE) % SIDE
        column = pl.multiple_of(((p * NC + core) * SIDE + block) * 256, 256)
        value = jnp.zeros((256, 256), jnp.float32)
        for m in range(pairs // 256):
            value = value + jnp.dot(
                back_t[m], counts[m * 256:m * 256 + 256, pl.ds(column, 256)],
                preferred_element_type=jnp.float32,
            )
        grad[p, core, torus.block(p, d)] = value.T.reshape(RING, 8, WIDTH)

    result = scatter_all(torus, chunk, grad, total, core_in, ring_in, mid_in, inner_in, sender)
    for p in PARTS:
        square = jnp.sum(result[p] * result[p], axis=1, keepdims=True)
        root = jnp.sqrt(mine[2, :, p * BLOCK:p * BLOCK + BLOCK] + square / WIDTH)
        root = jnp.concatenate([root, root], axis=1)
        out[p, c, torus.column(p) + torus.z] = mine[p] - learn_rate * result[p] / root
    for _ in gather_all(torus, out, sender):
        pass
    sender.drain()


def step(promote, ids, state, table, out_grad, weight_in, weight_out):
    f_count, l_count, samples = ids.shape
    pairs = f_count * samples
    hot_rows = 32 * BLOCK
    count = SCATTER_COPIES + 2 * GATHER_COPIES + 3
    tile = (8, WIDTH)
    f32, bf16, i32 = jnp.float32, jnp.bfloat16, jnp.int32
    scalar, vmem, hbm = (pl.BlockSpec(memory_space=m) for m in (pltpu.SMEM, pltpu.VMEM, pltpu.HBM))
    return pl.pallas_call(
        step_kernel,
        out_shape=(pltpu.VMEM(TILES, f32), pltpu.SMEM(promote.shape, i32)),
        in_specs=[scalar] + [hbm] * 6,
        out_specs=(vmem, scalar),
        scratch_shapes=[
            pltpu.VMEM(ids.shape, i32),
            pltpu.VMEM(state.shape, f32),
            pltpu.VMEM((table.shape[0], 16, WIDTH), f32),
            pltpu.VMEM((4, 3) + tile, f32),
            pltpu.VMEM((4, 3) + tile, f32),
            pltpu.VMEM((3,) + tile, f32),
            pltpu.VMEM(TILES, f32),
            pltpu.VMEM(out_grad.shape, bf16),
            pltpu.VMEM(weight_in.shape, bf16),
            pltpu.VMEM(weight_out.shape, bf16),
            pltpu.VMEM((f_count * l_count, samples), i32),
            pltpu.VMEM((pairs // 16, 256), i32),
            pltpu.VMEM((pairs // 16, 256), i32),
            pltpu.VMEM((pairs, hot_rows), bf16),
            pltpu.VMEM((hot_rows, WIDTH), bf16),
            pltpu.VMEM((pairs, WIDTH), f32),
            pltpu.VMEM((samples, weight_in.shape[1]), f32),
            pltpu.VMEM((pairs // 256, 256, 256), bf16),
            pltpu.VMEM(TILES, f32),
            pltpu.VMEM((2, CHIPS) + tile, f32),
            pltpu.VMEM((2, CHIPS) + tile, f32),
            pltpu.VMEM((2, 6, RING // 2) + tile, f32),
            pltpu.VMEM((2, 3, NZ) + tile, f32),
            pltpu.VMEM((2, 7) + tile, f32),
            pltpu.SemaphoreType.DMA((6,)),
            pltpu.SemaphoreType.DMA((count,)),
            pltpu.SemaphoreType.DMA((count,)),
        ],
        compiler_params=pltpu.CompilerParams(
            collective_id=0, has_side_effects=True, vmem_limit_bytes=56 * MIB
        ),
        name="step",
    )(promote, ids, state, table, out_grad, weight_in, weight_out)


WRITE_PIECES = 8


def write_kernel(order_ref, promote_ref, demote_ref, tiles, table_ref, out_hbm, table_hbm, out, patches, sems, patch_sems):
    per_piece = out.shape[0] // WRITE_PIECES

    def rows_of(q, n, h):
        ylo, z, c = q // 16, q // 2 % 8, q % 2
        x, y = n % 4, (n // 4) * 2 + ylo
        a, b = (y, x) if h else (x, y)
        return tiles[h, c, (a * SIDE + b) * NZ + z]

    table_copy = pltpu.make_async_copy(table_ref, table_hbm, sems.at[WRITE_PIECES])
    table_copy.start()

    def send(i):
        rows = pl.ds(pl.multiple_of(i * per_piece, per_piece), per_piece)
        return pltpu.make_async_copy(out.at[rows, :], out_hbm.at[rows, :], sems.at[i])

    def piece(i, carry):
        def one(k, carry):
            s = i * (per_piece // BLOCK) + k
            q = order_ref[s]
            dropped = demote_ref[0] == s
            for j in range(1, demote_ref.shape[0]):
                dropped = jnp.logical_or(dropped, demote_ref[j] == s)
            for n in range(8):
                for h in range(2):
                    first = pl.multiple_of(s * BLOCK + n * 16 + h * 8, 8)
                    out[pl.ds(first, 8), :] = jnp.where(dropped, 0.0, rows_of(q, n, h))
            return carry

        lax.fori_loop(0, per_piece // BLOCK, one, 0)
        send(i).start()
        return carry

    lax.fori_loop(0, WRITE_PIECES, piece, 0)

    count = table_ref.shape[0] // BLOCK
    first_block = lax.axis_index("table") * count
    slots = [demote_ref[j] for j in range(demote_ref.shape[0])]
    locals_ = [promote_ref[s] - first_block for s in slots]
    mine = [jnp.logical_and(local >= 0, local < count) for local in locals_]

    def patch(j):
        row = pl.multiple_of(jnp.clip(locals_[j], 0, count - 1) * BLOCK, BLOCK)
        return pltpu.make_async_copy(patches.at[j], table_hbm.at[pl.ds(row, BLOCK), :], patch_sems.at[j])

    table_copy.wait()
    for j in range(len(slots)):
        @pl.when(mine[j])
        def _():
            q = order_ref[slots[j]]
            for n in range(8):
                for h in range(2):
                    patches[j, n * 16 + h * 8:n * 16 + h * 8 + 8, :] = rows_of(q, n, h)
            patch(j).start()
    for j in range(len(slots)):
        @pl.when(mine[j])
        def _():
            patch(j).wait()
    for i in range(WRITE_PIECES):
        send(i).wait()


def write(order, promote, demote, tiles, table):
    scalar, vmem, hbm = (pl.BlockSpec(memory_space=m) for m in (pltpu.SMEM, pltpu.VMEM, pl.ANY))
    hot_rows = 32 * BLOCK
    return pl.pallas_call(
        write_kernel,
        out_shape=(
            jax.ShapeDtypeStruct((hot_rows, WIDTH), jnp.float32),
            jax.ShapeDtypeStruct(table.shape, jnp.float32),
        ),
        in_specs=[scalar] * 3 + [vmem, vmem],
        out_specs=(hbm, hbm),
        scratch_shapes=[
            pltpu.VMEM((hot_rows, WIDTH), jnp.float32),
            pltpu.VMEM((demote.shape[0], BLOCK, WIDTH), jnp.float32),
            pltpu.SemaphoreType.DMA((WRITE_PIECES + 1,)),
            pltpu.SemaphoreType.DMA((demote.shape[0],)),
        ],
        compiler_params=pltpu.CompilerParams(vmem_limit_bytes=24 * MIB),
        name="write",
    )(order, promote, demote, tiles, table)


def on_device(
    table_rows, accumulator, pooled_replica_rows, out_grad, weight_in, weight_out, promote, demote
):
    blk_count = table_rows.shape[0] // BLOCK
    ids = jnp.transpose(pooled_replica_rows, (1, 2, 0))
    tiles, order = step(
        promote, ids, accumulator.reshape(blk_count, BLOCK),
        table_rows.reshape(blk_count, 8, 16, WIDTH), out_grad, weight_in, weight_out,
    )
    replica_out, table_out = write(order, promote, demote, tiles, table_rows)
    return (table_out, replica_out)


def solution(mesh):
    placed = (
        P("table", None),
        P("table"),
        P(("node", "table"), None, None),
        P(("node", "table"), None),
        P(),
        P(),
        P(),
        P(),
    )
    return jax.shard_map(
        on_device, mesh=mesh, in_specs=placed, out_specs=(P("table", None), P()), check_vma=False
    )
```

```python
import jax
import jax.numpy as jnp
from jax import lax
from jax.experimental import pallas as pl
from jax.experimental.pallas import tpu as pltpu
from jax.sharding import PartitionSpec as P

MESH = pl.DeviceIdType.MESH
BLOCK = 128
NX, NY, NZ, NC = 4, 4, 8, 2
SIDE = 4
RING = NY * NZ
CHIPS = NX * RING
WIDTH = 256
TILES = (2, NC, CHIPS, 8, WIDTH)
FAR_FIRST = (4, 3, 5, 2, 6, 1, 7)
learn_rate = 0.5
MIB = 1 << 20
NT = (((1,), (1,)), ((), ()))


def device(x, y, z, c):
    return ((y // 2) * NX + x, (y % 2) * (NZ * NC) + z * NC + c)


class Torus:
    def __init__(self):
        self.node = lax.axis_index("node")
        self.table = lax.axis_index("table")
        yhi, self.x = self.node // NX, self.node % NX
        ylo, rest = self.table // (NZ * NC), self.table % (NZ * NC)
        self.y, self.z, self.c = yhi * 2 + ylo, rest // NC, rest % NC
        self.outer = (self.x, self.y)
        self.middle = (self.y, self.x)

    def along_x(self, d):
        return device((self.x + d + NX) % NX, self.y, self.z, self.c)

    def along_y(self, d):
        return device(self.x, (self.y + d + NY) % NY, self.z, self.c)

    def along_z(self, d):
        return device(self.x, self.y, (self.z + d) % NZ, self.c)

    def along_outer(self, p, d):
        return self.along_y(d) if p else self.along_x(d)

    def along_middle(self, p, d):
        return self.along_x(d) if p else self.along_y(d)

    def partner(self):
        return device(self.x, self.y, self.z, 1 - self.c)

    def column(self, p, d=0):
        return (self.outer[p] * SIDE + (self.middle[p] + d) % SIDE) * NZ

    def block(self, p, d, half=None):
        first = ((self.outer[p] + d + SIDE) % SIDE) * RING
        if half is None:
            return pl.ds(first, RING)
        return pl.ds(first + half * (RING // 2), RING // 2)

    def greet(self, more):
        sem = pltpu.get_barrier_semaphore()
        others = [self.along_x(d) for d in range(1, NX)]
        others += [self.along_y(d) for d in range(1, NY)]
        others += [self.along_z(d) for d in range(1, NZ)]
        others += [self.partner()] + more
        for other in others:
            pl.semaphore_signal(sem, inc=1, device_id=other, device_id_type=MESH)
        return sem, len(others)


class Sender:
    def __init__(self, send, recv):
        self.send, self.recv, self.next, self.all = send, recv, 0, []

    def start(self, src, dst, to):
        k = self.next
        self.next += 1
        copy = pltpu.make_async_remote_copy(
            src_ref=src, dst_ref=dst, send_sem=self.send.at[k], recv_sem=self.recv.at[k],
            device_id=to, device_id_type=MESH,
        )
        copy.start()
        self.all.append(copy)
        return copy

    def drain(self):
        for copy in self.all:
            copy.wait_send()


PARTS = (0, 1)


def gather_all(torus, out, sender):
    c = torus.c
    inner, middle, core, ring = {}, {}, {}, {}

    def forward(p, d):
        ref = out.at[p, c, torus.block(p, d)]
        core[p, d] = sender.start(ref, ref, torus.partner())

    def shift(p, d, half, way):
        ref = out.at[p, c, torus.block(p, d, half)]
        ring[p, d, half, way] = sender.start(ref, ref, torus.along_outer(p, way))

    for p in PARTS:
        ref = out.at[p, c, torus.column(p) + torus.z]
        inner[p] = [sender.start(ref, ref, torus.along_z(d)) for d in FAR_FIRST]
    yield "inner"
    for p in PARTS:
        for copy in inner[p]:
            copy.wait_recv()
        ref = out.at[p, c, pl.ds(torus.column(p), NZ)]
        middle[p] = [sender.start(ref, ref, torus.along_middle(p, d)) for d in range(1, SIDE)]
    yield "middle"
    for p in PARTS:
        for copy in middle[p]:
            copy.wait_recv()
        shift(p, 0, 0, 1)
        shift(p, 0, 1, -1)
        shift(p, 0, 1, 1)
        shift(p, 0, 0, -1)
        forward(p, 0)
    yield "own"
    for p in PARTS:
        ring[p, 0, 0, 1].wait_recv()
        shift(p, -1, 0, 1)
        ring[p, 0, 1, -1].wait_recv()
        shift(p, 1, 1, -1)
    yield "turn"
    for p in PARTS:
        ring[p, 0, 1, 1].wait_recv()
        forward(p, -1)
        ring[p, 0, 0, -1].wait_recv()
        forward(p, 1)
        core[p, 0].wait_recv()
    yield "near"
    for p in PARTS:
        ring[p, -1, 0, 1].wait_recv()
        ring[p, 1, 1, -1].wait_recv()
        forward(p, 2)
        core[p, -1].wait_recv()
        core[p, 1].wait_recv()
    yield "far"
    for p in PARTS:
        core[p, 2].wait_recv()


GATHER_COPIES = 2 * (7 + 3 + 6 + 4)
SCATTER_COPIES = 2 * (4 + 6 + 3 + 7)


def scatter_all(torus, chunk, grad, total, core_in, ring_in, mid_in, inner_in, sender):
    c = torus.c
    core, ring = {}, {}

    def to_core(p, d):
        chunk(p, 1 - c, d)
        where = torus.block(p, d)
        core[p, d] = sender.start(grad.at[p, 1 - c, where], core_in.at[p, where], torus.partner())

    def add_core(p, d):
        core[p, d].wait_recv()
        where = torus.block(p, d)
        total[p, where] = grad[p, c, where] + core_in[p, where]

    def shift(p, d, half, way, spot):
        ring[p, spot] = sender.start(
            total.at[p, torus.block(p, d, half)], ring_in.at[p, spot], torus.along_outer(p, way)
        )

    def absorb(p, d, half, spot):
        ring[p, spot].wait_recv()
        where = torus.block(p, d, half)
        total[p, where] = total[p, where] + ring_in[p, spot]

    for p in PARTS:
        to_core(p, 2)
    for p in PARTS:
        chunk(p, c, 2)
    for d in (1, -1):
        to_core(0, d)
    to_core(1, 1)
    for p in PARTS:
        add_core(p, 2)
        shift(p, 2, 0, 1, 0)
        shift(p, 2, 1, -1, 1)
    to_core(1, -1)
    for p in PARTS:
        chunk(p, c, 1)
        chunk(p, c, -1)
        add_core(p, 1)
        shift(p, 1, 1, 1, 2)
        add_core(p, -1)
        shift(p, -1, 0, -1, 3)
    for p in PARTS:
        to_core(p, 0)
    for p in PARTS:
        chunk(p, c, 0)
    for p in PARTS:
        absorb(p, 1, 0, 0)
        shift(p, 1, 0, 1, 4)
        absorb(p, -1, 1, 1)
        shift(p, -1, 1, -1, 5)
    for p in PARTS:
        add_core(p, 0)
        absorb(p, 0, 1, 2)
        absorb(p, 0, 0, 3)
    middle, inner, result = {}, {}, []
    for p in PARTS:
        absorb(p, 0, 0, 4)
        absorb(p, 0, 1, 5)
        middle[p] = [
            sender.start(
                total.at[p, pl.ds(torus.column(p, d), NZ)], mid_in.at[p, d - 1], torus.along_middle(p, d)
            )
            for d in range(1, SIDE)
        ]
    for p in PARTS:
        for copy in middle[p]:
            copy.wait_recv()
        own = pl.ds(torus.column(p), NZ)
        total[p, own] = total[p, own] + mid_in[p, 0] + mid_in[p, 1] + mid_in[p, 2]
        inner[p] = [
            sender.start(
                total.at[p, torus.column(p) + (torus.z + d) % NZ], inner_in.at[p, d - 1], torus.along_z(d)
            )
            for d in FAR_FIRST
        ]
    for p in PARTS:
        for copy in inner[p]:
            copy.wait_recv()
        value = total[p, torus.column(p) + torus.z]
        for d in range(NZ - 1):
            value = value + inner_in[p, d]
        result.append(value)
    return result


def step_kernel(
    promote_ref, ids_hbm, state_hbm, table_hbm, grad_hbm, win_hbm, wout_hbm,
    out, order_ref,
    ids_in, state_in, rows, outgo, income, mine, hot, dout, win, wout, ids_s, key_s, lo_s, counts, low, pooled, back, back_t,
    grad, total, core_in, ring_in, mid_in, inner_in, sems, send, recv,
):
    torus = Torus()
    c, node, table = torus.c, torus.node, torus.table
    f_count, l_count, samples = ids_in.shape
    pairs = f_count * samples
    slots = order_ref.shape[0]
    sender = Sender(send, recv)
    first, here = (table // 4) * 4, table % 4
    pull = pltpu.make_async_copy(table_hbm.at[:, node], rows, sems.at[0])
    pull.start()
    sem, greeted = torus.greet([device(torus.x, torus.y, (torus.z // 2) * 2 + (1 - torus.z % 2), 1 - c)])
    small = [
        pltpu.make_async_copy(src, dst, sems.at[k])
        for k, src, dst in ((4, state_hbm, state_in), (5, ids_hbm, ids_in))
    ]
    loads = [
        pltpu.make_async_copy(src, dst, sems.at[k])
        for k, src, dst in ((1, grad_hbm, dout), (2, wout_hbm, wout), (3, win_hbm, win))
    ]
    for copy in small + loads:
        copy.start()

    blk_count = rows.shape[0]
    group = [jnp.int32(1 << 30)] * 4
    for s in range(slots):
        value = promote_ref[s]
        value = jnp.where(value // (4 * blk_count) == table // 4, value, 1 << 30)
        for j in range(4):
            group[j], value = jnp.minimum(group[j], value), jnp.maximum(group[j], value)
    pull.wait()
    small[0].wait()
    for j in range(4):
        local = jnp.clip(group[j] - table * blk_count, 0, blk_count - 1)
        block = rows[local]
        outgo[j, 0] = block[0:8]
        outgo[j, 1] = block[8:16]
        state = jnp.broadcast_to(state_in[pl.ds(local, 1), :], (8, BLOCK))
        outgo[j, 2, :, 0:BLOCK] = state
        outgo[j, 2, :, BLOCK:WIDTH] = state
    pl.semaphore_wait(sem, greeted)
    copies = [
        sender.start(outgo.at[(here + d) % 4], income.at[here], (node, first + (here + d) % 4))
        for d in range(1, 4)
    ]
    income[here] = outgo[here]

    for copy in copies:
        copy.wait_recv()
    kept = jnp.where(here == 0, group[0], jnp.where(here == 1, group[1], jnp.where(here == 2, group[2], group[3])))
    got = income[(kept // blk_count) % 4]
    lane = lax.broadcasted_iota(jnp.int32, (8, 128), 1)
    sub = lax.broadcasted_iota(jnp.int32, (8, 128), 0)
    for p in PARTS:
        hot[p, c, torus.column(p) + torus.z] = got[p]
        mine[p] = got[p]
        own = jnp.where(lane == node * 16 + p * 8 + sub, got[2, :, 0:BLOCK], 0.0)
        mine[2, :, p * BLOCK:p * BLOCK + BLOCK] = jnp.broadcast_to(
            jnp.sum(own, axis=1, keepdims=True), (8, BLOCK)
        )
    fetch = gather_all(torus, hot, sender)
    next(fetch)

    small[1].wait()
    ids = ids_in[...].reshape(f_count * l_count, samples)
    slot = ids >> 7
    block = jnp.zeros_like(slot)
    for s in range(slots):
        block = jnp.where(slot == s, promote_ref[s], block)
    q = jnp.zeros_like(slot)
    for s in range(slots):
        q = q + jnp.where(promote_ref[s] < block, 1, 0)
    ylo, base = q >> 4, (q & 1) * 1024 + ((q >> 1) & 7) * 8
    x = (ids >> 4) & 3
    y = ((ids >> 6) & 1) * 2 + ylo
    lower = ((ids >> 3) & 1) == 1
    place = jnp.where(lower, 2048 + y * 256 + x * 64, x * 256 + y * 64)
    ids_s[...] = base + place + (ids & 7)

    for f in range(f_count):
        for t in range(samples // 128):
            for half in range(2):
                row = jnp.zeros((8, 128), jnp.int32)
                for k in range(8):
                    l = half * 8 + k
                    one = jnp.broadcast_to(
                        ids_s[f * l_count + l:f * l_count + l + 1, t * 128:t * 128 + 128], (8, 128)
                    )
                    turned = pltpu.roll(one, 0, 1, stride=16, stride_axis=0)
                    turned = pltpu.roll(turned, k * 16, 1)
                    row = jnp.where(lane // 16 == k, turned, row)
                g = f * (samples // 16) + t * 8
                key_s[g:g + 8, half * 128:half * 128 + 128] = (row >> 8) * 16 + lane % 16
                lo_s[g:g + 8, half * 128:half * 128 + 128] = row & 255

    spot = lax.broadcasted_iota(jnp.int32, (256, 256), 0)

    def build(g, carry):
        key = key_s[pl.ds(g, 1), :]
        lo = lo_s[pl.ds(g, 1), :]
        one = jnp.where(spot == key, 1.0, 0.0).astype(jnp.bfloat16)
        two = jnp.where(spot == lo, 1.0, 0.0).astype(jnp.bfloat16)
        product = lax.dot_general(one, two, NT, preferred_element_type=jnp.float32).astype(jnp.bfloat16)
        row = pl.multiple_of((g // 8 * 8 + (8 - g % 8) % 8) * 16, 16)
        for hi in range(16):
            counts[pl.ds(row, 16), hi * 256:hi * 256 + 256] = product[hi * 16:hi * 16 + 16]
        return carry

    def pool(blocks, start=False):
        columns = []
        for p, core, d in blocks:
            block = (torus.outer[p] + d + SIDE) % SIDE
            column = pl.ds(pl.multiple_of(((p * NC + core) * SIDE + block) * 256, 256), 256)
            low[column, :] = hot[p, core, torus.block(p, d)].reshape(256, WIDTH).astype(jnp.bfloat16)
            columns.append(column)

        def one(m, carry):
            spots = pl.ds(pl.multiple_of(m * 256, 256), 256)
            value = None if start else pooled[spots, :]
            for column in columns:
                term = jnp.dot(counts[spots, column], low[column, :], preferred_element_type=jnp.float32)
                value = term if value is None else value + term
            pooled[spots, :] = value
            return carry

        lax.fori_loop(0, pairs // 256, one, 0, unroll=2)

    groups = pairs // 16
    early, late = groups // 4, groups * 5 // 8
    lax.fori_loop(0, early, build, 0, unroll=4)
    next(fetch)
    lax.fori_loop(early, late, build, 0, unroll=4)
    next(fetch)
    lax.fori_loop(late, groups, build, 0, unroll=4)
    loads[0].wait()
    loads[1].wait()

    def project(m, carry):
        spots = pl.ds(pl.multiple_of(m * 256, 256), 256)
        back[spots, :] = lax.dot_general(dout[spots, :], wout[...], NT, preferred_element_type=jnp.float32)
        return carry

    lax.fori_loop(0, samples // 256, project, 0)

    def rank(s, carry):
        total = jnp.int32(0)
        for other in range(slots):
            total = total + jnp.where(promote_ref[other] < promote_ref[s], 1, 0)
        order_ref[s] = total
        return carry

    lax.fori_loop(0, slots, rank, 0)
    next(fetch)
    pool([(p, c, 0) for p in PARTS], start=True)
    next(fetch)
    pool([(p, core, d) for p in PARTS for core, d in ((c, -1), (c, 1), (1 - c, 0))])
    next(fetch)
    pool([(p, core, d) for p in PARTS for core, d in ((c, 2), (1 - c, -1), (1 - c, 1))])
    next(fetch, None)
    pool([(p, 1 - c, 2) for p in PARTS])
    loads[2].wait()

    def dense(m, carry):
        start = pl.multiple_of(m * 256, 256)
        pre = jnp.zeros((256, win.shape[1]), jnp.float32)
        for f in range(f_count):
            part = pooled[pl.ds(pl.multiple_of(f * samples + start, 256), 256), :].astype(jnp.bfloat16)
            pre = pre + jnp.dot(part, win[f * 256:f * 256 + 256, :], preferred_element_type=jnp.float32)
        sig = jax.nn.sigmoid(pre)
        back_pre = (back[pl.ds(start, 256), :] * sig * (1.0 + pre * (1.0 - sig))).astype(jnp.bfloat16)
        for f in range(f_count):
            back_t[f * (samples // 256) + m] = lax.dot_general(
                win[f * 256:f * 256 + 256, :], back_pre, NT, preferred_element_type=jnp.float32
            ).astype(jnp.bfloat16)
        return carry

    lax.fori_loop(0, samples // 256, dense, 0, unroll=2)

    def chunk(p, core, d):
        block = (torus.outer[p] + d + SIDE) % SIDE
        column = pl.multiple_of(((p * NC + core) * SIDE + block) * 256, 256)
        value = jnp.zeros((256, 256), jnp.float32)
        for m in range(pairs // 256):
            value = value + jnp.dot(
                back_t[m], counts[m * 256:m * 256 + 256, pl.ds(column, 256)],
                preferred_element_type=jnp.float32,
            )
        grad[p, core, torus.block(p, d)] = value.T.reshape(RING, 8, WIDTH)

    result = scatter_all(torus, chunk, grad, total, core_in, ring_in, mid_in, inner_in, sender)
    for p in PARTS:
        square = jnp.sum(result[p] * result[p], axis=1, keepdims=True)
        root = jnp.sqrt(mine[2, :, p * BLOCK:p * BLOCK + BLOCK] + square / WIDTH)
        root = jnp.concatenate([root, root], axis=1)
        out[p, c, torus.column(p) + torus.z] = mine[p] - learn_rate * result[p] / root
    for _ in gather_all(torus, out, sender):
        pass
    sender.drain()


def step(promote, ids, state, table, out_grad, weight_in, weight_out):
    f_count, l_count, samples = ids.shape
    pairs = f_count * samples
    hot_rows = 32 * BLOCK
    count = SCATTER_COPIES + 2 * GATHER_COPIES + 3
    tile = (8, WIDTH)
    f32, bf16, i32 = jnp.float32, jnp.bfloat16, jnp.int32
    scalar, vmem, hbm = (pl.BlockSpec(memory_space=m) for m in (pltpu.SMEM, pltpu.VMEM, pltpu.HBM))
    return pl.pallas_call(
        step_kernel,
        out_shape=(pltpu.VMEM(TILES, f32), pltpu.SMEM(promote.shape, i32)),
        in_specs=[scalar] + [hbm] * 6,
        out_specs=(vmem, scalar),
        scratch_shapes=[
            pltpu.VMEM(ids.shape, i32),
            pltpu.VMEM(state.shape, f32),
            pltpu.VMEM((table.shape[0], 16, WIDTH), f32),
            pltpu.VMEM((4, 3) + tile, f32),
            pltpu.VMEM((4, 3) + tile, f32),
            pltpu.VMEM((3,) + tile, f32),
            pltpu.VMEM(TILES, f32),
            pltpu.VMEM(out_grad.shape, bf16),
            pltpu.VMEM(weight_in.shape, bf16),
            pltpu.VMEM(weight_out.shape, bf16),
            pltpu.VMEM((f_count * l_count, samples), i32),
            pltpu.VMEM((pairs // 16, 256), i32),
            pltpu.VMEM((pairs // 16, 256), i32),
            pltpu.VMEM((pairs, hot_rows), bf16),
            pltpu.VMEM((hot_rows, WIDTH), bf16),
            pltpu.VMEM((pairs, WIDTH), f32),
            pltpu.VMEM((samples, weight_in.shape[1]), f32),
            pltpu.VMEM((pairs // 256, 256, 256), bf16),
            pltpu.VMEM(TILES, f32),
            pltpu.VMEM((2, CHIPS) + tile, f32),
            pltpu.VMEM((2, CHIPS) + tile, f32),
            pltpu.VMEM((2, 6, RING // 2) + tile, f32),
            pltpu.VMEM((2, 3, NZ) + tile, f32),
            pltpu.VMEM((2, 7) + tile, f32),
            pltpu.SemaphoreType.DMA((6,)),
            pltpu.SemaphoreType.DMA((count,)),
            pltpu.SemaphoreType.DMA((count,)),
        ],
        compiler_params=pltpu.CompilerParams(
            collective_id=0, has_side_effects=True, vmem_limit_bytes=56 * MIB
        ),
        name="step",
    )(promote, ids, state, table, out_grad, weight_in, weight_out)


WRITE_PIECES = 8


def write_kernel(order_ref, promote_ref, demote_ref, tiles, table_ref, out_hbm, table_hbm, out, patches, sems, patch_sems):
    per_piece = out.shape[0] // WRITE_PIECES

    def rows_of(q):
        ylo, z, c = q // 16, q // 2 % 8, q % 2
        upper = tiles.at[0, c, pl.ds(ylo * NZ + z, 113)]
        lower = tiles.at[1, c, pl.ds(ylo * RING + z, 89)]
        for n in range(8):
            x, yhi = n % 4, n // 4
            yield n * 16, upper[(x * SIDE + yhi * 2) * NZ]
            yield n * 16 + 8, lower[(yhi * 2 * SIDE + x) * NZ]

    table_copy = pltpu.make_async_copy(table_ref, table_hbm, sems.at[WRITE_PIECES])
    table_copy.start()

    def send(i):
        rows = pl.ds(pl.multiple_of(i * per_piece, per_piece), per_piece)
        return pltpu.make_async_copy(out.at[rows, :], out_hbm.at[rows, :], sems.at[i])

    def piece(i, carry):
        def one(k, carry):
            s = i * (per_piece // BLOCK) + k
            q = order_ref[s]
            dropped = demote_ref[0] == s
            for j in range(1, demote_ref.shape[0]):
                dropped = jnp.logical_or(dropped, demote_ref[j] == s)
            block = out.at[pl.ds(pl.multiple_of(s * BLOCK, BLOCK), BLOCK), :]
            for first, value in rows_of(q):
                block[first:first + 8, :] = jnp.where(dropped, 0.0, value)
            return carry

        lax.fori_loop(0, per_piece // BLOCK, one, 0)
        send(i).start()
        return carry

    lax.fori_loop(0, WRITE_PIECES // 2, piece, 0)

    count = table_ref.shape[0] // BLOCK
    first_block = lax.axis_index("table") * count
    slots = [demote_ref[j] for j in range(demote_ref.shape[0])]
    locals_ = [promote_ref[s] - first_block for s in slots]
    mine = [jnp.logical_and(local >= 0, local < count) for local in locals_]

    def patch(j):
        row = pl.multiple_of(jnp.clip(locals_[j], 0, count - 1) * BLOCK, BLOCK)
        return pltpu.make_async_copy(patches.at[j], table_hbm.at[pl.ds(row, BLOCK), :], patch_sems.at[j])

    table_copy.wait()
    for j in range(len(slots)):
        @pl.when(mine[j])
        def _():
            for first, value in rows_of(order_ref[slots[j]]):
                patches[j, first:first + 8, :] = value
            patch(j).start()
    lax.fori_loop(WRITE_PIECES // 2, WRITE_PIECES, piece, 0)
    for j in range(len(slots)):
        @pl.when(mine[j])
        def _():
            patch(j).wait()
    for i in range(WRITE_PIECES):
        send(i).wait()


def write(order, promote, demote, tiles, table):
    scalar, vmem, hbm = (pl.BlockSpec(memory_space=m) for m in (pltpu.SMEM, pltpu.VMEM, pl.ANY))
    hot_rows = 32 * BLOCK
    return pl.pallas_call(
        write_kernel,
        out_shape=(
            jax.ShapeDtypeStruct((hot_rows, WIDTH), jnp.float32),
            jax.ShapeDtypeStruct(table.shape, jnp.float32),
        ),
        in_specs=[scalar] * 3 + [vmem, vmem],
        out_specs=(hbm, hbm),
        scratch_shapes=[
            pltpu.VMEM((hot_rows, WIDTH), jnp.float32),
            pltpu.VMEM((demote.shape[0], BLOCK, WIDTH), jnp.float32),
            pltpu.SemaphoreType.DMA((WRITE_PIECES + 1,)),
            pltpu.SemaphoreType.DMA((demote.shape[0],)),
        ],
        compiler_params=pltpu.CompilerParams(vmem_limit_bytes=24 * MIB),
        name="write",
    )(order, promote, demote, tiles, table)


def on_device(
    table_rows, accumulator, pooled_replica_rows, out_grad, weight_in, weight_out, promote, demote
):
    blk_count = table_rows.shape[0] // BLOCK
    ids = jnp.transpose(pooled_replica_rows, (1, 2, 0))
    tiles, order = step(
        promote, ids, accumulator.reshape(blk_count, BLOCK),
        table_rows.reshape(blk_count, 8, 16, WIDTH), out_grad, weight_in, weight_out,
    )
    replica_out, table_out = write(order, promote, demote, tiles, table_rows)
    return (table_out, replica_out)


def solution(mesh):
    placed = (
        P("table", None),
        P("table"),
        P(("node", "table"), None, None),
        P(("node", "table"), None),
        P(),
        P(),
        P(),
        P(),
    )
    return jax.shard_map(
        on_device, mesh=mesh, in_specs=placed, out_specs=(P("table", None), P()), check_vma=False
    )
```

```python
import jax
import jax.numpy as jnp
from jax import lax
from jax.experimental import pallas as pl
from jax.experimental.pallas import tpu as pltpu
from jax.sharding import PartitionSpec as P

MESH = pl.DeviceIdType.MESH
BLOCK = 128
NX, NY, NZ, NC = 4, 4, 8, 2
SIDE = 4
RING = NY * NZ
CHIPS = NX * RING
WIDTH = 256
TILES = (2, NC, CHIPS, 8, WIDTH)
FAR_FIRST = (4, 3, 5, 2, 6, 1, 7)
learn_rate = 0.5
MIB = 1 << 20
NT = (((1,), (1,)), ((), ()))


def device(x, y, z, c):
    return ((y // 2) * NX + x, (y % 2) * (NZ * NC) + z * NC + c)


class Torus:
    def __init__(self):
        self.node = lax.axis_index("node")
        self.table = lax.axis_index("table")
        yhi, self.x = self.node // NX, self.node % NX
        ylo, rest = self.table // (NZ * NC), self.table % (NZ * NC)
        self.y, self.z, self.c = yhi * 2 + ylo, rest // NC, rest % NC
        self.outer = (self.x, self.y)
        self.middle = (self.y, self.x)

    def along_x(self, d):
        return device((self.x + d + NX) % NX, self.y, self.z, self.c)

    def along_y(self, d):
        return device(self.x, (self.y + d + NY) % NY, self.z, self.c)

    def along_z(self, d):
        return device(self.x, self.y, (self.z + d) % NZ, self.c)

    def along_outer(self, p, d):
        return self.along_y(d) if p else self.along_x(d)

    def along_middle(self, p, d):
        return self.along_x(d) if p else self.along_y(d)

    def partner(self):
        return device(self.x, self.y, self.z, 1 - self.c)

    def column(self, p, d=0):
        return (self.outer[p] * SIDE + (self.middle[p] + d) % SIDE) * NZ

    def block(self, p, d, half=None):
        first = ((self.outer[p] + d + SIDE) % SIDE) * RING
        if half is None:
            return pl.ds(first, RING)
        return pl.ds(first + half * (RING // 2), RING // 2)

    def greet(self, more):
        sem = pltpu.get_barrier_semaphore()
        others = [self.along_x(d) for d in range(1, NX)]
        others += [self.along_y(d) for d in range(1, NY)]
        others += [self.along_z(d) for d in range(1, NZ)]
        others += [self.partner()] + more
        for other in others:
            pl.semaphore_signal(sem, inc=1, device_id=other, device_id_type=MESH)
        return sem, len(others)


class Sender:
    def __init__(self, send, recv):
        self.send, self.recv, self.next, self.all = send, recv, 0, []

    def start(self, src, dst, to):
        k = self.next
        self.next += 1
        copy = pltpu.make_async_remote_copy(
            src_ref=src, dst_ref=dst, send_sem=self.send.at[k], recv_sem=self.recv.at[k],
            device_id=to, device_id_type=MESH,
        )
        copy.start()
        self.all.append(copy)
        return copy

    def drain(self):
        for copy in self.all:
            copy.wait_send()


PARTS = (0, 1)


def gather_all(torus, out, sender):
    c = torus.c
    inner, middle, core, ring = {}, {}, {}, {}

    def forward(p, d):
        ref = out.at[p, c, torus.block(p, d)]
        core[p, d] = sender.start(ref, ref, torus.partner())

    def shift(p, d, half, way):
        ref = out.at[p, c, torus.block(p, d, half)]
        ring[p, d, half, way] = sender.start(ref, ref, torus.along_outer(p, way))

    for p in PARTS:
        ref = out.at[p, c, torus.column(p) + torus.z]
        inner[p] = [sender.start(ref, ref, torus.along_z(d)) for d in FAR_FIRST]
    yield "inner"
    for p in PARTS:
        for copy in inner[p]:
            copy.wait_recv()
        ref = out.at[p, c, pl.ds(torus.column(p), NZ)]
        middle[p] = [sender.start(ref, ref, torus.along_middle(p, d)) for d in range(1, SIDE)]
    yield "middle"
    for p in PARTS:
        for copy in middle[p]:
            copy.wait_recv()
        shift(p, 0, 0, 1)
        shift(p, 0, 1, -1)
        shift(p, 0, 1, 1)
        shift(p, 0, 0, -1)
        forward(p, 0)
    yield "own"
    for p in PARTS:
        ring[p, 0, 0, 1].wait_recv()
        shift(p, -1, 0, 1)
        ring[p, 0, 1, -1].wait_recv()
        shift(p, 1, 1, -1)
    yield "turn"
    for p in PARTS:
        ring[p, 0, 1, 1].wait_recv()
        forward(p, -1)
        ring[p, 0, 0, -1].wait_recv()
        forward(p, 1)
        core[p, 0].wait_recv()
    yield "near"
    for p in PARTS:
        ring[p, -1, 0, 1].wait_recv()
        ring[p, 1, 1, -1].wait_recv()
        forward(p, 2)
        core[p, -1].wait_recv()
        core[p, 1].wait_recv()
    yield "far"
    for p in PARTS:
        core[p, 2].wait_recv()


GATHER_COPIES = 2 * (7 + 3 + 6 + 4)
SCATTER_COPIES = 2 * (4 + 6 + 3 + 7)


def scatter_all(torus, chunk, grad, total, core_in, ring_in, mid_in, inner_in, sender):
    c = torus.c
    core, ring = {}, {}

    def to_core(p, d):
        chunk(p, 1 - c, d)
        where = torus.block(p, d)
        core[p, d] = sender.start(grad.at[p, 1 - c, where], core_in.at[p, where], torus.partner())

    def add_core(p, d):
        core[p, d].wait_recv()
        where = torus.block(p, d)
        total[p, where] = grad[p, c, where] + core_in[p, where]

    def shift(p, d, half, way, spot):
        ring[p, spot] = sender.start(
            total.at[p, torus.block(p, d, half)], ring_in.at[p, spot], torus.along_outer(p, way)
        )

    def absorb(p, d, half, spot):
        ring[p, spot].wait_recv()
        where = torus.block(p, d, half)
        total[p, where] = total[p, where] + ring_in[p, spot]

    for p in PARTS:
        to_core(p, 2)
    for p in PARTS:
        chunk(p, c, 2)
    for d in (1, -1):
        to_core(0, d)
    to_core(1, 1)
    for p in PARTS:
        add_core(p, 2)
        shift(p, 2, 0, 1, 0)
        shift(p, 2, 1, -1, 1)
    to_core(1, -1)
    for p in PARTS:
        chunk(p, c, 1)
        chunk(p, c, -1)
        add_core(p, 1)
        shift(p, 1, 1, 1, 2)
        add_core(p, -1)
        shift(p, -1, 0, -1, 3)
    for p in PARTS:
        to_core(p, 0)
    for p in PARTS:
        chunk(p, c, 0)
    for p in PARTS:
        absorb(p, 1, 0, 0)
        shift(p, 1, 0, 1, 4)
        absorb(p, -1, 1, 1)
        shift(p, -1, 1, -1, 5)
    for p in PARTS:
        add_core(p, 0)
        absorb(p, 0, 1, 2)
        absorb(p, 0, 0, 3)
    middle, inner, result = {}, {}, []
    for p in PARTS:
        absorb(p, 0, 0, 4)
        absorb(p, 0, 1, 5)
        middle[p] = [
            sender.start(
                total.at[p, pl.ds(torus.column(p, d), NZ)], mid_in.at[p, d - 1], torus.along_middle(p, d)
            )
            for d in range(1, SIDE)
        ]
    for p in PARTS:
        for copy in middle[p]:
            copy.wait_recv()
        own = pl.ds(torus.column(p), NZ)
        total[p, own] = total[p, own] + mid_in[p, 0] + mid_in[p, 1] + mid_in[p, 2]
        inner[p] = [
            sender.start(
                total.at[p, torus.column(p) + (torus.z + d) % NZ], inner_in.at[p, d - 1], torus.along_z(d)
            )
            for d in FAR_FIRST
        ]
    for p in PARTS:
        for copy in inner[p]:
            copy.wait_recv()
        value = total[p, torus.column(p) + torus.z]
        for d in range(NZ - 1):
            value = value + inner_in[p, d]
        result.append(value)
    return result


def step_kernel(
    promote_ref, ids_hbm, state_hbm, table_hbm, grad_hbm, win_hbm, wout_hbm,
    out, order_ref,
    ids_in, state_in, rows, outgo, income, mine, hot, dout, win, wout, ids_s, key_s, lo_s, counts, low, pooled, back, back_t,
    grad, total, core_in, ring_in, mid_in, inner_in, sems, send, recv,
):
    torus = Torus()
    c, node, table = torus.c, torus.node, torus.table
    f_count, l_count, samples = ids_in.shape
    pairs = f_count * samples
    slots = order_ref.shape[0]
    sender = Sender(send, recv)
    first, here = (table // 4) * 4, table % 4
    pull = pltpu.make_async_copy(table_hbm.at[:, node], rows, sems.at[0])
    pull.start()
    sem, greeted = torus.greet([device(torus.x, torus.y, (torus.z // 2) * 2 + (1 - torus.z % 2), 1 - c)])
    small = [
        pltpu.make_async_copy(src, dst, sems.at[k])
        for k, src, dst in ((4, state_hbm, state_in), (5, ids_hbm, ids_in))
    ]
    loads = [
        pltpu.make_async_copy(src, dst, sems.at[k])
        for k, src, dst in ((1, grad_hbm, dout), (2, wout_hbm, wout), (3, win_hbm, win))
    ]
    for copy in small + loads:
        copy.start()

    blk_count = rows.shape[0]
    group = [jnp.int32(1 << 30)] * 4
    for s in range(slots):
        value = promote_ref[s]
        value = jnp.where(value // (4 * blk_count) == table // 4, value, 1 << 30)
        for j in range(4):
            group[j], value = jnp.minimum(group[j], value), jnp.maximum(group[j], value)
    pull.wait()
    small[0].wait()
    for j in range(4):
        local = jnp.clip(group[j] - table * blk_count, 0, blk_count - 1)
        block = rows[local]
        outgo[j, 0] = block[0:8]
        outgo[j, 1] = block[8:16]
        state = jnp.broadcast_to(state_in[pl.ds(local, 1), :], (8, BLOCK))
        outgo[j, 2, :, 0:BLOCK] = state
        outgo[j, 2, :, BLOCK:WIDTH] = state
    pl.semaphore_wait(sem, greeted)
    copies = [
        sender.start(outgo.at[(here + d) % 4], income.at[here], (node, first + (here + d) % 4))
        for d in range(1, 4)
    ]
    income[here] = outgo[here]

    for copy in copies:
        copy.wait_recv()
    kept = jnp.where(here == 0, group[0], jnp.where(here == 1, group[1], jnp.where(here == 2, group[2], group[3])))
    got = income[(kept // blk_count) % 4]
    lane = lax.broadcasted_iota(jnp.int32, (8, 128), 1)
    sub = lax.broadcasted_iota(jnp.int32, (8, 128), 0)
    for p in PARTS:
        hot[p, c, torus.column(p) + torus.z] = got[p]
        mine[p] = got[p]
        own = jnp.where(lane == node * 16 + p * 8 + sub, got[2, :, 0:BLOCK], 0.0)
        mine[2, :, p * BLOCK:p * BLOCK + BLOCK] = jnp.broadcast_to(
            jnp.sum(own, axis=1, keepdims=True), (8, BLOCK)
        )
    fetch = gather_all(torus, hot, sender)
    next(fetch)

    small[1].wait()
    ids = ids_in[...].reshape(f_count * l_count, samples)
    slot = ids >> 7
    block = jnp.zeros_like(slot)
    for s in range(slots):
        block = jnp.where(slot == s, promote_ref[s], block)
    q = jnp.zeros_like(slot)
    for s in range(slots):
        q = q + jnp.where(promote_ref[s] < block, 1, 0)
    ylo, base = q >> 4, (q & 1) * 1024 + ((q >> 1) & 7) * 8
    x = (ids >> 4) & 3
    y = ((ids >> 6) & 1) * 2 + ylo
    lower = ((ids >> 3) & 1) == 1
    place = jnp.where(lower, 2048 + y * 256 + x * 64, x * 256 + y * 64)
    ids_s[...] = base + place + (ids & 7)

    for f in range(f_count):
        for t in range(samples // 128):
            for half in range(2):
                row = jnp.zeros((8, 128), jnp.int32)
                for k in range(8):
                    l = half * 8 + k
                    one = jnp.broadcast_to(
                        ids_s[f * l_count + l:f * l_count + l + 1, t * 128:t * 128 + 128], (8, 128)
                    )
                    turned = pltpu.roll(one, 0, 1, stride=16, stride_axis=0)
                    turned = pltpu.roll(turned, k * 16, 1)
                    row = jnp.where(lane // 16 == k, turned, row)
                g = f * (samples // 16) + t * 8
                key_s[g:g + 8, half * 128:half * 128 + 128] = (row >> 8) * 16 + lane % 16
                lo_s[g:g + 8, half * 128:half * 128 + 128] = row & 255

    spot = lax.broadcasted_iota(jnp.int32, (256, 256), 0)

    def build(g, carry):
        key = key_s[pl.ds(g, 1), :]
        lo = lo_s[pl.ds(g, 1), :]
        one = jnp.where(spot == key, 1.0, 0.0).astype(jnp.bfloat16)
        two = jnp.where(spot == lo, 1.0, 0.0).astype(jnp.bfloat16)
        product = lax.dot_general(one, two, NT, preferred_element_type=jnp.float32).astype(jnp.bfloat16)
        row = pl.multiple_of((g // 8 * 8 + (8 - g % 8) % 8) * 16, 16)
        for hi in range(16):
            counts[pl.ds(row, 16), hi * 256:hi * 256 + 256] = product[hi * 16:hi * 16 + 16]
        return carry

    def lowered(blocks):
        columns = []
        for p, core, d in blocks:
            block = (torus.outer[p] + d + SIDE) % SIDE
            column = pl.ds(pl.multiple_of(((p * NC + core) * SIDE + block) * 256, 256), 256)
            low[column, :] = hot[p, core, torus.block(p, d)].reshape(256, WIDTH).astype(jnp.bfloat16)
            columns.append(column)
        return columns

    def pool(blocks, start=False):
        columns = lowered(blocks)

        def one(m, carry):
            spots = pl.ds(pl.multiple_of(m * 256, 256), 256)
            value = None if start else pooled[spots, :]
            for column in columns:
                term = jnp.dot(counts[spots, column], low[column, :], preferred_element_type=jnp.float32)
                value = term if value is None else value + term
            pooled[spots, :] = value
            return carry

        lax.fori_loop(0, pairs // 256, one, 0, unroll=2)

    groups = pairs // 16
    early, late = groups // 4, groups * 5 // 8
    lax.fori_loop(0, early, build, 0, unroll=4)
    next(fetch)
    lax.fori_loop(early, late, build, 0, unroll=4)
    next(fetch)
    lax.fori_loop(late, groups, build, 0, unroll=4)
    loads[0].wait()
    loads[1].wait()

    def project(m, carry):
        spots = pl.ds(pl.multiple_of(m * 256, 256), 256)
        back[spots, :] = lax.dot_general(dout[spots, :], wout[...], NT, preferred_element_type=jnp.float32)
        return carry

    lax.fori_loop(0, samples // 256, project, 0)

    def rank(s, carry):
        total = jnp.int32(0)
        for other in range(slots):
            total = total + jnp.where(promote_ref[other] < promote_ref[s], 1, 0)
        order_ref[s] = total
        return carry

    lax.fori_loop(0, slots, rank, 0)
    next(fetch)
    pool([(p, c, 0) for p in PARTS], start=True)
    next(fetch)
    pool([(p, core, d) for p in PARTS for core, d in ((c, -1), (c, 1), (1 - c, 0))])
    next(fetch)
    pool([(p, core, d) for p in PARTS for core, d in ((c, 2), (1 - c, -1), (1 - c, 1))])
    next(fetch, None)
    last = lowered([(p, 1 - c, 2) for p in PARTS])
    loads[2].wait()

    def dense(m, carry):
        start = pl.multiple_of(m * 256, 256)
        pre = jnp.zeros((256, win.shape[1]), jnp.float32)
        for f in range(f_count):
            spots = pl.ds(pl.multiple_of(f * samples + start, 256), 256)
            part = pooled[spots, :]
            for column in last:
                part = part + jnp.dot(counts[spots, column], low[column, :], preferred_element_type=jnp.float32)
            part = part.astype(jnp.bfloat16)
            pre = pre + jnp.dot(part, win[f * 256:f * 256 + 256, :], preferred_element_type=jnp.float32)
        sig = jax.nn.sigmoid(pre)
        back_pre = (back[pl.ds(start, 256), :] * sig * (1.0 + pre * (1.0 - sig))).astype(jnp.bfloat16)
        for f in range(f_count):
            back_t[f * (samples // 256) + m] = lax.dot_general(
                win[f * 256:f * 256 + 256, :], back_pre, NT, preferred_element_type=jnp.float32
            ).astype(jnp.bfloat16)
        return carry

    lax.fori_loop(0, samples // 256, dense, 0, unroll=2)

    def chunk(p, core, d):
        block = (torus.outer[p] + d + SIDE) % SIDE
        column = pl.multiple_of(((p * NC + core) * SIDE + block) * 256, 256)
        value = jnp.zeros((256, 256), jnp.float32)
        for m in range(pairs // 256):
            value = value + jnp.dot(
                back_t[m], counts[m * 256:m * 256 + 256, pl.ds(column, 256)],
                preferred_element_type=jnp.float32,
            )
        grad[p, core, torus.block(p, d)] = value.T.reshape(RING, 8, WIDTH)

    result = scatter_all(torus, chunk, grad, total, core_in, ring_in, mid_in, inner_in, sender)
    for p in PARTS:
        square = jnp.sum(result[p] * result[p], axis=1, keepdims=True)
        root = jnp.sqrt(mine[2, :, p * BLOCK:p * BLOCK + BLOCK] + square / WIDTH)
        root = jnp.concatenate([root, root], axis=1)
        out[p, c, torus.column(p) + torus.z] = mine[p] - learn_rate * result[p] / root
    for _ in gather_all(torus, out, sender):
        pass
    sender.drain()


def step(promote, ids, state, table, out_grad, weight_in, weight_out):
    f_count, l_count, samples = ids.shape
    pairs = f_count * samples
    hot_rows = 32 * BLOCK
    count = SCATTER_COPIES + 2 * GATHER_COPIES + 3
    tile = (8, WIDTH)
    f32, bf16, i32 = jnp.float32, jnp.bfloat16, jnp.int32
    scalar, vmem, hbm = (pl.BlockSpec(memory_space=m) for m in (pltpu.SMEM, pltpu.VMEM, pltpu.HBM))
    return pl.pallas_call(
        step_kernel,
        out_shape=(pltpu.VMEM(TILES, f32), pltpu.SMEM(promote.shape, i32)),
        in_specs=[scalar] + [hbm] * 6,
        out_specs=(vmem, scalar),
        scratch_shapes=[
            pltpu.VMEM(ids.shape, i32),
            pltpu.VMEM(state.shape, f32),
            pltpu.VMEM((table.shape[0], 16, WIDTH), f32),
            pltpu.VMEM((4, 3) + tile, f32),
            pltpu.VMEM((4, 3) + tile, f32),
            pltpu.VMEM((3,) + tile, f32),
            pltpu.VMEM(TILES, f32),
            pltpu.VMEM(out_grad.shape, bf16),
            pltpu.VMEM(weight_in.shape, bf16),
            pltpu.VMEM(weight_out.shape, bf16),
            pltpu.VMEM((f_count * l_count, samples), i32),
            pltpu.VMEM((pairs // 16, 256), i32),
            pltpu.VMEM((pairs // 16, 256), i32),
            pltpu.VMEM((pairs, hot_rows), bf16),
            pltpu.VMEM((hot_rows, WIDTH), bf16),
            pltpu.VMEM((pairs, WIDTH), f32),
            pltpu.VMEM((samples, weight_in.shape[1]), f32),
            pltpu.VMEM((pairs // 256, 256, 256), bf16),
            pltpu.VMEM(TILES, f32),
            pltpu.VMEM((2, CHIPS) + tile, f32),
            pltpu.VMEM((2, CHIPS) + tile, f32),
            pltpu.VMEM((2, 6, RING // 2) + tile, f32),
            pltpu.VMEM((2, 3, NZ) + tile, f32),
            pltpu.VMEM((2, 7) + tile, f32),
            pltpu.SemaphoreType.DMA((6,)),
            pltpu.SemaphoreType.DMA((count,)),
            pltpu.SemaphoreType.DMA((count,)),
        ],
        compiler_params=pltpu.CompilerParams(
            collective_id=0, has_side_effects=True, vmem_limit_bytes=56 * MIB
        ),
        name="step",
    )(promote, ids, state, table, out_grad, weight_in, weight_out)


WRITE_PIECES = 8


def write_kernel(order_ref, promote_ref, demote_ref, tiles, table_ref, out_hbm, table_hbm, out, patches, sems, patch_sems):
    per_piece = out.shape[0] // WRITE_PIECES

    def rows_of(q):
        ylo, z, c = q // 16, q // 2 % 8, q % 2
        upper = tiles.at[0, c, pl.ds(ylo * NZ + z, 113)]
        lower = tiles.at[1, c, pl.ds(ylo * RING + z, 89)]
        for n in range(8):
            x, yhi = n % 4, n // 4
            yield n * 16, upper[(x * SIDE + yhi * 2) * NZ]
            yield n * 16 + 8, lower[(yhi * 2 * SIDE + x) * NZ]

    table_copy = pltpu.make_async_copy(table_ref, table_hbm, sems.at[WRITE_PIECES])
    table_copy.start()

    def send(i):
        rows = pl.ds(pl.multiple_of(i * per_piece, per_piece), per_piece)
        return pltpu.make_async_copy(out.at[rows, :], out_hbm.at[rows, :], sems.at[i])

    def piece(i, carry):
        def one(k, carry):
            s = i * (per_piece // BLOCK) + k
            q = order_ref[s]
            dropped = demote_ref[0] == s
            for j in range(1, demote_ref.shape[0]):
                dropped = jnp.logical_or(dropped, demote_ref[j] == s)
            block = out.at[pl.ds(pl.multiple_of(s * BLOCK, BLOCK), BLOCK), :]
            for first, value in rows_of(q):
                block[first:first + 8, :] = jnp.where(dropped, 0.0, value)
            return carry

        lax.fori_loop(0, per_piece // BLOCK, one, 0)
        send(i).start()
        return carry

    lax.fori_loop(0, WRITE_PIECES // 2, piece, 0)

    count = table_ref.shape[0] // BLOCK
    first_block = lax.axis_index("table") * count
    slots = [demote_ref[j] for j in range(demote_ref.shape[0])]
    locals_ = [promote_ref[s] - first_block for s in slots]
    mine = [jnp.logical_and(local >= 0, local < count) for local in locals_]

    def patch(j):
        row = pl.multiple_of(jnp.clip(locals_[j], 0, count - 1) * BLOCK, BLOCK)
        return pltpu.make_async_copy(patches.at[j], table_hbm.at[pl.ds(row, BLOCK), :], patch_sems.at[j])

    table_copy.wait()
    for j in range(len(slots)):
        @pl.when(mine[j])
        def _():
            for first, value in rows_of(order_ref[slots[j]]):
                patches[j, first:first + 8, :] = value
            patch(j).start()
    lax.fori_loop(WRITE_PIECES // 2, WRITE_PIECES, piece, 0)
    for j in range(len(slots)):
        @pl.when(mine[j])
        def _():
            patch(j).wait()
    for i in range(WRITE_PIECES):
        send(i).wait()


def write(order, promote, demote, tiles, table):
    scalar, vmem, hbm = (pl.BlockSpec(memory_space=m) for m in (pltpu.SMEM, pltpu.VMEM, pl.ANY))
    hot_rows = 32 * BLOCK
    return pl.pallas_call(
        write_kernel,
        out_shape=(
            jax.ShapeDtypeStruct((hot_rows, WIDTH), jnp.float32),
            jax.ShapeDtypeStruct(table.shape, jnp.float32),
        ),
        in_specs=[scalar] * 3 + [vmem, vmem],
        out_specs=(hbm, hbm),
        scratch_shapes=[
            pltpu.VMEM((hot_rows, WIDTH), jnp.float32),
            pltpu.VMEM((demote.shape[0], BLOCK, WIDTH), jnp.float32),
            pltpu.SemaphoreType.DMA((WRITE_PIECES + 1,)),
            pltpu.SemaphoreType.DMA((demote.shape[0],)),
        ],
        compiler_params=pltpu.CompilerParams(vmem_limit_bytes=24 * MIB),
        name="write",
    )(order, promote, demote, tiles, table)


def on_device(
    table_rows, accumulator, pooled_replica_rows, out_grad, weight_in, weight_out, promote, demote
):
    blk_count = table_rows.shape[0] // BLOCK
    ids = jnp.transpose(pooled_replica_rows, (1, 2, 0))
    tiles, order = step(
        promote, ids, accumulator.reshape(blk_count, BLOCK),
        table_rows.reshape(blk_count, 8, 16, WIDTH), out_grad, weight_in, weight_out,
    )
    replica_out, table_out = write(order, promote, demote, tiles, table_rows)
    return (table_out, replica_out)


def solution(mesh):
    placed = (
        P("table", None),
        P("table"),
        P(("node", "table"), None, None),
        P(("node", "table"), None),
        P(),
        P(),
        P(),
        P(),
    )
    return jax.shard_map(
        on_device, mesh=mesh, in_specs=placed, out_specs=(P("table", None), P()), check_vma=False
    )
```
